128 devices in a mesh: row: 16 (over z_lo, y, core), col: 8 (over x, z_hi).
Axes of the slice: x: 4, y: 4, z: 4 (z_hi: 2, z_lo: 2; z = z_hi * 2 + z_lo), core: 2. Of those that a mesh axis runs over, the one named last changes fastest.
Arguments:
- weights: bfloat16 [32768, 1024], P(('row', 'col')), may hold values from -6 to 6
- tile_pattern: int32 [128, 2], P(('row', 'col')), may hold values 0 or 1
Outputs:
- similarity: bfloat16 [32768, 32768], P('row', 'col')
The draws below stay inside these ranges and needn't reach their ends.
Inputs may be any that keep to these rules, and one draw needn't show every extreme that they name: `tile_pattern`: 1 where the tile holds weights, 0 where it is empty.
All inputs are finite; a program needn't handle non-finite values. No bound on the sum of `tile_pattern` on one device may be relied on, other than what follows from the above.
Results may differ from the reference program's by a relative error of at most 0.001.
Values may be sent and summed in bfloat16 or wider, within the bound.
A program may use at most 128 MiB of HBM per device.

```python
import math
import jax
import jax.numpy as jnp
from jax import lax

RT = 256
BT = 512
SECTIONS = 2
BINS = 1024
READS = 32768


def touch_ends(entries, own_key, least, largest):
    shape = entries.shape
    spot = [jax.random.randint(jax.random.fold_in(own_key, axis), (), 0, shape[axis]) for axis in range(len(shape))]
    entries = entries.at[tuple(spot)].set(least)
    longest = shape.index(max(shape))
    spot[longest] = (spot[longest] + 1) % shape[longest]
    return entries.at[tuple(spot)].set(largest)


def levels(stream_key, shape, cuts, least, largest):
    loudness = 1.0
    for position, blocks in cuts:
        steps = jax.random.uniform(jax.random.fold_in(jax.random.fold_in(stream_key, 6), position), (blocks,), jnp.float32, least / len(cuts), largest / len(cuts))
        loudness = loudness * jnp.repeat(jnp.exp(steps), shape[position] // blocks).reshape((-1,) + (1,) * (len(shape) - 1 - position))
    return loudness


def bell_draw(stream_key, shape, scale, limit, split=(), kind=jnp.bfloat16):
    values = scale * jax.random.normal(stream_key, shape, jnp.float32)
    if split:
        values = values * levels(stream_key, shape, split, -0.22, 0.18)
    return jnp.clip(values, -limit, limit).astype(kind)


def setup_inputs(seed: int = 0) -> dict:
    keys = jax.random.split(jax.random.key(seed), 3)
    return {
        "weights": bell_draw(keys[0], (READS, BINS), 1.0, 6.0, ((0, 128),)),
        "tile_pattern": touch_ends((jax.random.randint(keys[1], (READS // RT, SECTIONS), 0, 2) < 1).astype(jnp.int32), jax.random.fold_in(keys[1], 1), 0, 1),
    }


def reference(weights, tile_pattern):
    tile_mask = jnp.repeat(tile_pattern, RT, axis=0).astype(jnp.bfloat16)
    masked = (weights.reshape(READS, SECTIONS, BT) * tile_mask[:, :, None]).reshape(READS, BINS)
    block_rows = min(READS, 2048)
    scale = 1.0 / math.sqrt(BINS)
    col_ids = jnp.arange(READS, dtype=jnp.int32)

    def one_block(block_index):
        row_slab = lax.dynamic_slice_in_dim(masked, block_index * block_rows, block_rows, 0)
        product = lax.dot_general(row_slab, masked, (((1,), (1,)), ((), ())), preferred_element_type=jnp.float32)
        row_ids = block_index * block_rows + jnp.arange(block_rows, dtype=jnp.int32)
        same = row_ids[:, None] == col_ids[None, :]
        return jnp.where(same, jnp.float32(0.0), product * jnp.float32(scale)).astype(jnp.bfloat16)
    blocks = lax.map(one_block, jnp.arange(READS // block_rows, dtype=jnp.int32))
    return blocks.reshape(READS, READS)
```

```python
import math

import jax
import jax.numpy as jnp
from jax import lax
from jax.experimental import pallas as pl
from jax.experimental.pallas import tpu as pltpu
from jax.sharding import PartitionSpec as P

MESH = pl.DeviceIdType.MESH
CHUNKS = 4
SLOTS = (
    (
        (0,0,((0,0,1,2,3,6),(0,1,0,1,5,6),(0,2,0,1,4,6),(0,3,0,2,3,6))),
        (0,1,((1,0,1),(1,1,0,1),(1,2,0,1,2),(1,3,0,1))),
        (0,2,((2,0,1),(2,1,0,1,2),(2,2,0,1),(2,3,0,1,2))),
        (0,3,((3,0,2),(3,1,0,1,2),(3,2,0,1,2),(3,3,0,1))),
        (0,4,((4,0,1,2),(4,1,0,2),(4,2,0,1,2),(4,3,1))),
        (0,5,((5,0,1,2),(5,1,0),(5,2,0,1,2),(5,3,0,2))),
        (0,6,((6,0,0,2),(6,1,0,2),(6,2,0,1),(6,3,1))),
        (0,7,((7,0,0,1),(7,1,0,1),(7,2,0,1),(7,3,0,1,2))),
    ),
    (
        (0,0,((1,0,1,2,5,6),(3,1,4,6))),
        (0,1,((0,1,2),(2,0,1,2))),
        (0,2,((1,1,0,2),(3,1,2))),
        (0,3,((0,0),(2,1))),
        (0,4,((5,0,1,2),(7,0,2))),
        (0,5,((4,1,0,2),(6,2,2))),
        (0,6,((5,1,2),(7,0,2))),
        (0,7,((4,0),(6,0))),
        (1,1,((0,0,3,5,6),)),
        (1,3,((0,2,4,5,6),)),
    ),
    (
        (0,0,((4,0,0,3,6),)),
        (0,1,((5,0),)),
        (0,2,((6,0,0),)),
        (0,3,((7,3,0),)),
        (0,4,((0,0,0),)),
        (0,5,((1,2,0),)),
        (0,6,((2,1,0,1),)),
        (0,7,((3,0,0,1),)),
        (1,4,((0,1,3,4,6),)),
    ),
    (
        (0,0,((1,1,2,4,6),(3,2,0,5,6))),
        (0,1,((0,2,0,2),(2,1))),
        (0,2,((1,2,0),(3,2))),
        (0,3,((0,1,1,2),(2,2,0))),
        (0,4,((5,2),(7,1))),
        (0,5,((4,2),(6,3,1,2))),
        (0,6,((5,2,0,2),(7,1,1,2))),
        (0,7,((4,2),(6,1,2))),
        (1,1,((0,3,3,6),)),
    ),
    (
        (0,0,((4,1,1,3,6),)),
        (0,1,((5,2,1),)),
        (0,2,((6,1,1),)),
        (0,4,((0,3),)),
        (0,6,((2,3,1),)),
        (0,7,((3,1),)),
        (1,2,((0,0,3,6),(0,2,4,5,6))),
        (1,3,((3,1,4,5,6),)),
    ),
    (
        (0,0,((1,2,3,6),(3,3,2,4,6))),
        (0,1,((0,3,0),(2,2,2))),
        (0,2,((1,3),(3,3,2))),
        (0,3,((0,2),(2,3,2))),
        (0,4,((7,2,2),)),
        (0,5,((0,0,2,0),(2,0,0,1),(2,1))),
        (0,6,((5,3,0),(7,2,1))),
        (0,7,((4,3,1,2),(6,2,0))),
        (1,1,((4,0,3,5,6),)),
        (1,4,((1,0,3,4,6),)),
        (1,5,((0,0,4,6),(0,1,5,6))),
        (1,7,((0,1,5,4,6),(0,2,3,6))),
    ),
    (
        (0,0,((4,2,1,5,6),)),
        (0,1,((5,3,1),)),
        (0,2,((7,0),)),
        (0,4,((1,0,0),(6,3,1))),
        (0,6,((1,1),)),
        (0,7,((3,2,0,1),)),
        (1,2,((0,3,5,6),)),
        (1,3,((1,1,4,5,6),)),
    ),
    (
        (0,0,((1,3,2,5,6),(7,3,4,6))),
        (0,1,((2,3,1),(4,0,0))),
        (0,2,((0,1),(0,2,2))),
        (0,3,((1,0,1,2),(1,1,2),(6,1,0))),
        (0,4,((7,3,0),)),
        (0,5,((7,1),(0,1,1,0))),
        (0,6,((4,1,0),(7,3,2))),
        (0,7,((2,1,0),(5,0,2))),
        (1,1,((4,1,3,5,6),)),
    ),
    (
        (0,0,((5,0,3,6),)),
        (0,1,((4,1),)),
        (0,2,((5,1,0),)),
        (0,4,((1,1,0),)),
        (0,6,((3,1,1),)),
        (0,7,((0,1),)),
        (1,1,((0,2,6),)),
        (1,2,((3,1,4,6),)),
        (1,3,((0,0,6),)),
        (1,4,((3,2,3,4,6),(0,0,4,6),(0,2,6))),
        (1,5,((1,0,5,3,6),)),
        (1,6,((0,1,5,6),(0,2,4,6))),
        (1,7,((1,0,5,6),(3,1,3,4,6))),
    ),
    (
        (0,0,((2,0,1,3,6),(2,2,4,6))),
        (0,1,((3,2,2),(6,1,2))),
        (0,2,((0,3,0,2),)),
        (0,3,((4,1,1),(6,0,0))),
        (0,4,((2,0,1),(3,0,2,0))),
        (0,5,((2,3,1),)),
        (0,6,((1,2),(3,0,2))),
        (0,7,((5,2,2),)),
        (1,1,((0,1,6),)),
        (1,2,((4,0,3,5,6),)),
        (1,3,((3,3,4,5,6),(0,1,6))),
        (1,5,((4,0,4,6),)),
    ),
    (
        (0,3,((4,3,0),)),
        (0,5,((0,2,1),(1,0,0))),
        (0,7,((6,3),)),
        (1,1,((1,2,3,5,6),)),
        (1,2,((1,1,4,6),)),
    ),
    (
        (0,0,((7,0,1,0,5,6),)),
        (0,1,((6,2,0),)),
        (0,2,((1,0),(7,1,1))),
        (0,4,((3,3,1),(0,1))),
        (0,6,((3,3,1),)),
        (0,7,((2,3),)),
        (1,2,((4,1,3,6),)),
        (1,3,((7,3,4,6),)),
        (1,4,((4,2,3,4,6),)),
        (1,5,((3,2,5,3,6),)),
        (1,6,((0,3,4,3,6),)),
        (1,7,((1,1,3,4,6),(3,2,6))),
    ),
    (
        (0,0,((5,2,3,6),(6,1,2,4,6))),
        (0,2,((4,0,2,0),)),
        (0,3,((1,2,2),(4,2,1),(5,0,1))),
        (0,4,((6,2,2),)),
        (0,5,((7,2,2),(7,3),(2,2,0,1))),
        (0,6,((2,0),(4,3,1))),
        (0,7,((5,3,0),(2,0))),
        (1,1,((3,1,6),(5,0,3,5,6))),
        (1,2,((3,3,4,6),)),
        (1,3,((4,0,6),)),
        (1,4,((3,1,6),)),
        (1,5,((4,1,4,3,6),(0,2,6))),
        (1,6,((1,0,5,6),(3,1,4,6))),
    ),
    (
        (0,0,((7,2,1,5,6),)),
        (0,1,((6,3,0,1),)),
        (0,2,((4,1),(5,2))),
        (0,4,((2,3),(1,3,1))),
        (0,6,((0,2),)),
        (0,7,((1,0),)),
        (1,1,((1,0,6),)),
        (1,2,((0,1,6),(1,2,3,6))),
        (1,3,((1,0,6),(2,2,4,5,6))),
        (1,4,((4,0,6),(1,3,3,4,6))),
    ),
    (
        (0,0,((5,3,1,3,6),(6,0,2,0,4,6))),
        (0,3,((2,0),(5,1,2,0),(5,2))),
        (0,4,((3,2),)),
        (0,5,((3,1,2,1),(1,1))),
        (0,6,((0,0,2,0),(3,2))),
        (0,7,((4,1),)),
        (1,1,((1,1,6),(2,0,3,6))),
        (1,5,((4,2,5,3,6),)),
        (1,6,((4,0,3,6),)),
        (1,7,((0,0,4,6),(3,3,3,4,6))),
    ),
    (
        (0,1,((7,0,2),(7,1,1))),
        (0,2,((6,2,0),(4,2,2,1))),
        (0,5,((3,2),)),
        (0,7,((3,3),)),
        (1,2,((7,3,4,5,6),)),
        (1,3,((4,1,6),(6,1,4,5,6))),
        (1,4,((1,1,6),)),
        (1,5,((1,2,4,3,6),(0,3,4,6))),
        (1,6,((1,1,4,6),(3,2,5,6))),
        (1,7,((0,3,5,6),)),
    ),
    (
        (0,0,((3,0,3,6),(2,3,5,6),(4,3,0,4,6))),
        (0,1,((0,0),)),
        (0,2,((7,3,1),)),
        (0,3,((0,3,2),(7,0))),
        (0,4,((0,2,1),(2,1,2),(6,1))),
        (0,5,((3,3,2),)),
        (0,6,((0,3,1),(0,1))),
        (0,7,((1,1),)),
        (1,1,((3,2,6),(3,3,6))),
        (1,2,((5,0,3,6),)),
        (1,4,((4,1,6),(7,0,3,4,6))),
        (1,7,((4,2,6),)),
    ),
    (
        (0,2,((6,3,0),)),
        (0,5,((3,0),(6,1))),
        (0,7,((1,3,2,1),)),
        (1,1,((5,2,3,5,6),)),
        (1,2,((1,0,6),(2,2,4,6))),
        (1,3,((1,2,6),)),
        (1,5,((1,3,5,6),(3,1,6))),
        (1,6,((0,0,6),(4,1,3,6))),
        (1,7,((2,2,3,4,6),)),
    ),
    (
        (0,0,((5,1,2,0,4,6),(6,3,3,5,6),(6,2,4,5,6))),
        (0,1,((6,0),(7,2,0))),
        (0,2,((5,0,2),(3,0,1))),
        (0,3,((4,0),(7,2))),
        (0,4,((2,2),(5,3))),
        (0,5,((4,3),)),
        (0,6,((1,0),(4,0,1))),
        (0,7,((0,0),(1,2,0))),
        (1,1,((7,3,6),)),
        (1,2,((2,0,5,6),)),
        (1,3,((6,0,4,5,6),)),
        (1,4,((3,3,6),)),
        (1,5,((5,0,4,3,6),)),
        (1,7,((4,0,6),(1,3,5,4,6))),
    ),
    (
        (0,1,((4,2),)),
        (0,4,((6,0,0),)),
        (0,7,((0,2),)),
        (1,1,((4,2,6),(5,3,3,5,6))),
        (1,2,((6,1,4,6),)),
        (1,4,((1,2,6),(7,2,3,4,6))),
        (1,6,((7,3,4,3,6),)),
    ),
    (
        (0,1,((4,3,0),)),
        (0,4,((3,1),)),
        (0,5,((7,0),)),
        (1,2,((3,2,3,6),(5,2,3,5,6))),
        (1,3,((0,3,6),(5,0,6),(4,3,4,5,6))),
        (1,5,((1,1,6),(7,0,5,3,6))),
        (1,6,((3,3,4,6),(4,2,5,6))),
        (1,7,((6,1,3,4,6),(7,0,5,6))),
    ),
    (
        (0,0,((7,1,1,4,5,6),(2,1,3,4,5,6))),
        (0,1,((3,1),(7,3))),
        (0,2,((0,0),)),
        (0,3,((5,3,1),(6,2))),
        (0,5,((0,3),)),
        (0,6,((2,2,0),(4,2),(1,3,1))),
        (0,7,((5,1),)),
        (1,1,((2,2,6),(3,0,3,5,6))),
        (1,2,((6,0,4,6),)),
        (1,4,((0,3,6),(2,2,6))),
        (1,5,((5,2,4,6),)),
        (1,7,((4,1,6),)),
    ),
    (
        (0,1,((5,1),)),
        (0,2,((7,2),)),
        (0,3,((1,3),)),
        (0,4,((1,2),)),
        (0,5,((6,0),)),
        (1,1,((1,3,6),)),
        (1,3,((5,1,4,5,6),)),
        (1,4,((2,3,3,4,6),)),
        (1,6,((1,2,3,6),(2,2,4,6))),
    ),
    (
        (0,1,((3,3),)),
        (0,3,((6,3),)),
        (0,4,((5,1),)),
        (0,5,((4,0),)),
        (0,6,((5,0),)),
        (0,7,((0,3),)),
        (1,1,((6,1,6),(6,3,3,6))),
        (1,2,((5,3,3,6),)),
        (1,3,((1,3,6),(3,2,6))),
        (1,4,((5,0,6),)),
        (1,5,((7,3,6),(7,2,5,3,6))),
        (1,6,((2,0,4,3,6),)),
        (1,7,((7,2,5,6),(6,0,3,4,6),(7,3,3,6))),
    ),
    (
        (0,1,((3,0),)),
        (0,2,((5,3),(4,3))),
        (0,3,((7,1),)),
        (0,7,((2,2),)),
        (1,2,((4,3,4,6),(4,2,3,6))),
        (1,3,((6,2,4,6),)),
        (1,4,((6,1,3,6),)),
        (1,5,((5,3,4,3,6),)),
        (1,6,((1,3,5,6),(5,0,3,6))),
    ),
    (
        (0,5,((1,3),)),
        (1,1,((7,0,6),(6,0,6))),
        (1,2,((3,0,3,5,6),)),
        (1,3,((7,0,6),)),
        (1,4,((6,3,3,4,6),)),
        (1,5,((3,3,6),)),
    ),
    (
        (1,1,((2,1,5,6),)),
        (1,2,((5,1,4,6),)),
        (1,3,((5,2,6),)),
        (1,4,((5,2,6),)),
        (1,5,((2,3,5,3,6),)),
        (1,6,((5,2,3,6),(6,1,6),(7,0,5,6))),
        (1,7,((1,2,6),(2,3,5,6),(4,3,3,4,6))),
    ),
    (
        (1,1,((4,3,6),(7,2,6))),
        (1,2,((6,3,3,6),)),
        (1,3,((7,1,4,5,6),)),
        (1,4,((6,0,6),)),
        (1,5,((3,0,4,6),(2,2,6))),
    ),
    (
        (1,2,((6,2,4,5,6),)),
        (1,3,((5,3,6),(7,2,6))),
        (1,4,((5,3,4,6),(6,2,3,4,6))),
        (1,5,((6,1,6),)),
        (1,7,((2,0,5,6),)),
    ),
    (
        (1,2,((1,3,6),)),
        (1,3,((2,1,4,5,6),)),
        (1,4,((7,3,6),)),
        (1,5,((2,0,4,6),)),
        (1,6,((6,0,4,6),(7,2,5,6),(3,0,3,6))),
        (1,7,((6,3,4,6),(5,1,3,4,6))),
    ),
    (
        (1,1,((5,1,5,6),(2,3,6))),
        (1,2,((7,1,4,5,6),)),
        (1,3,((4,2,6),)),
        (1,5,((2,1,3,6),(6,3,6))),
        (1,7,((5,0,6),)),
    ),
    (
        (1,2,((7,0,6),)),
        (1,3,((2,3,4,6),)),
        (1,4,((3,0,6),(7,1,3,6))),
        (1,6,((4,3,4,6),(5,3,6))),
    ),
    (
        (1,1,((6,2,6),)),
        (1,3,((3,0,6),)),
        (1,4,((4,3,6),)),
        (1,5,((6,0,6),)),
        (1,6,((6,2,6),)),
        (1,7,((5,3,6),(7,1,6),(5,2,6))),
    ),
    (
        (1,2,((2,1,6),)),
        (1,4,((2,0,6),)),
        (1,5,((6,2,6),)),
        (1,6,((2,3,6),(6,3,6))),
    ),
    (
        (1,1,((7,1,6),)),
        (1,2,((7,2,6),)),
        (1,3,((2,0,6),)),
        (1,4,((5,1,6),(2,1,6))),
        (1,5,((5,1,6),)),
        (1,7,((6,2,6),)),
    ),
    (
        (1,2,((2,3,6),)),
        (1,3,((6,3,6),)),
        (1,5,((4,3,6),(7,1,6))),
        (1,6,((2,1,6),(5,1,6),(7,1,6))),
        (1,7,((3,0,6),(2,1,6))),
    ),
)
XP, XM, ZH, YP, YM, ZL, CORE = range(7)


def place():
    row, col = lax.axis_index("row"), lax.axis_index("col")
    return col // 2, lax.rem(col, 2), lax.rem(row // 2, 4), row // 8, lax.rem(row, 2)


def device(x, zh, y, zl, core):
    return (zl * 8 + y * 2 + core, x * 2 + zh)


def neighbours(x, zh, y, zl, core):
    def turn(a, by):
        return lax.rem(a + by, 4)

    return {
        XP: device(turn(x, 1), zh, y, zl, core),
        XM: device(turn(x, 3), zh, y, zl, core),
        ZH: device(x, 1 - zh, y, zl, core),
        YP: device(x, zh, turn(y, 1), zl, core),
        YM: device(x, zh, turn(y, 3), zl, core),
        ZL: device(x, zh, y, 1 - zl, core),
        CORE: device(x, zh, y, zl, 1 - core),
    }


def flip(a, b):
    return a + b - 2 * a * b


def gather_kernel(pattern_ref, weights_ref, left, right, send_sems, row_sems, col_sems, core_sem, local_sem):
    reads, bins = weights_ref.shape
    section_count = pattern_ref.shape[1]
    bin_tile = bins // section_count
    piece = reads // CHUNKS
    x, zh, y, zl, core = place()
    near = neighbours(x, zh, y, zl, core)
    barrier = pltpu.get_barrier_semaphore()
    for target in near.values():
        pl.semaphore_signal(barrier, inc=1, device_id=target, device_id_type=MESH)
    own = pl.multiple_of((x * 2 + zh) * reads, reads)
    for section in range(section_count):
        part = pl.ds(section * bin_tile, bin_tile)
        keep = pattern_ref[0, section].astype(jnp.float32)
        left[pl.ds(own, reads), part] = (weights_ref[:, part].astype(jnp.float32) * keep).astype(left.dtype)
    pl.semaphore_wait(barrier, len(near))

    row_root = (2 * zl + y // 2, lax.rem(y, 2))
    col_root = (2 * lax.rem(x, 2) + zh, x // 2)
    row_place = lax.rem(x - row_root[0] + 4, 4) + 4 * flip(zh, row_root[1])
    col_place = lax.rem(y - col_root[0] + 4, 4) + 4 * flip(zl, col_root[1])
    row_source = [lax.rem(row_root[0] + s % 4, 4) * 2 + flip(row_root[1], s // 4) for s in range(8)]
    col_source = [lax.rem(x + s % 4, 4) * 2 + flip(zh, s // 4) for s in range(8)]
    row_tile = [pl.multiple_of(a * reads, reads) for a in row_source]
    col_tile = [pl.multiple_of((core * 8 + a) * reads, reads) for a in col_source]

    def in_left(s, c):
        return left.at[pl.ds(row_tile[s] + c * piece, piece)]

    def in_right(s, c):
        return right.at[pl.ds(col_tile[s] + c * piece, piece)]

    def copy(src, dst, way, recv_sem):
        return pltpu.make_async_remote_copy(
            src_ref=src, dst_ref=dst, send_sem=send_sems.at[way], recv_sem=recv_sem, device_id=near[way], device_id_type=MESH
        )

    def handle(kind, role, s, c, ways):
        row_sem = row_sems.at[row_source[s], c]
        col_sem = col_sems.at[col_source[s], c]
        if kind == 0:
            src = in_left(s, c)
            if s != role:
                copy(src, src, XP, row_sem).wait_recv()
        else:
            src = in_right(s, c)
            copy(src, src, YP, col_sem).wait_recv()
        for way in ways:
            if way <= ZH:
                copy(src, src, way, row_sem).start()
            elif way <= ZL:
                copy(src, in_right(s, c), way, col_sem).start()
            else:
                copy(src, in_right(s, c), way, core_sem).start()
        if kind == 0 and role == 0:
            pltpu.make_async_copy(src, in_right(s, c), local_sem).start()

    sent = {}
    for slot in SLOTS:
        for kind, role, entries in slot:
            for entry in entries:
                for way in entry[2:]:
                    at = (0 if way <= ZH else 1, role, way)
                    sent[at] = sent.get(at, 0) + 1

            @pl.when((row_place if kind == 0 else col_place) == role)
            def _(kind=kind, role=role, entries=entries):
                for entry in entries:
                    handle(kind, role, entry[0], entry[1], entry[2:])

    def held(count):
        return right.at[pl.ds(0, count * piece)]

    for (kind, role, way), count in sorted(sent.items()):
        if way == CORE:
            continue

        @pl.when((row_place if kind == 0 else col_place) == role)
        def _(way=way, count=count):
            copy(held(count), held(count), way, core_sem).wait_send()

    every = held(8 * CHUNKS)

    @pl.when(col_place == 0)
    def _():
        pltpu.make_async_copy(every, every, local_sem).wait()

    copy(every, every, CORE, core_sem).wait()


def gather(tile_pattern, weights):
    reads, bins = weights.shape
    return pl.pallas_call(
        gather_kernel,
        out_shape=(pltpu.VMEM((8 * reads, bins), weights.dtype), pltpu.VMEM((16 * reads, bins), weights.dtype)),
        in_specs=[pl.BlockSpec(memory_space=pltpu.SMEM), pl.BlockSpec(memory_space=pltpu.VMEM)],
        out_specs=(pl.BlockSpec(memory_space=pltpu.VMEM), pl.BlockSpec(memory_space=pltpu.VMEM)),
        scratch_shapes=[
            pltpu.SemaphoreType.DMA((7,)),
            pltpu.SemaphoreType.DMA((8, CHUNKS)),
            pltpu.SemaphoreType.DMA((8, CHUNKS)),
            pltpu.SemaphoreType.DMA,
            pltpu.SemaphoreType.DMA,
        ],
        compiler_params=pltpu.CompilerParams(collective_id=0, has_side_effects=True, vmem_limit_bytes=8 << 20),
        name="gather",
    )(tile_pattern, weights)


def product_kernel(scale, left, right, out, left_full, right_full, stage, sems):
    bin_tile = left.shape[1] // left_full.shape[1]
    tile = stage.shape[1]
    rows, cols = left.shape[0] // tile, right.shape[0] // tile
    sections = left_full.shape[1]

    def look(array, full, count):
        @pl.loop(0, count)
        def _(i):
            at = pl.ds(pl.multiple_of(i * tile, tile), tile)
            for s in range(sections):
                top = jnp.max(jnp.abs(array[at, pl.ds(s * bin_tile, bin_tile)]).astype(jnp.float32))
                full[i, s] = (top > 0.0).astype(jnp.int32)

    look(left, left_full, rows)
    look(right, right_full, cols)
    first_row = lax.axis_index("row") * rows
    first_col = lax.axis_index("col") * cols

    def write(i, slot):
        return pltpu.make_async_copy(stage.at[slot], out.at[pl.ds(pl.multiple_of(i * tile, tile), tile)], sems.at[slot])

    @pl.loop(0, rows)
    def _(i):
        slot = lax.rem(i, 2)

        @pl.when(i >= 2)
        def _():
            write(i - 2, slot).wait()

        lhs = pl.ds(pl.multiple_of(i * tile, tile), tile)

        @pl.loop(0, cols)
        def _(j):
            at = pl.ds(pl.multiple_of(j * tile, tile), tile)
            case = left_full[i, 0] * right_full[j, 0] + 2 * left_full[i, 1] * right_full[j, 1]

            def put(part):
                acc = lax.dot_general(left[lhs, part], right[at, part], (((1,), (1,)), ((), ())), preferred_element_type=jnp.float32)
                stage[slot, :, at] = (acc * scale).astype(stage.dtype)

            @pl.when(case == 0)
            def _():
                stage[slot, :, at] = jnp.zeros((tile, tile), stage.dtype)

            @pl.when(case == 1)
            def _():
                put(pl.ds(0, bin_tile))

            @pl.when(case == 2)
            def _():
                put(pl.ds(bin_tile, bin_tile))

            @pl.when(case == 3)
            def _():
                put(pl.ds(0, 2 * bin_tile))

            @pl.when(first_row + i == first_col + j)
            def _():
                shape = (tile, tile)
                same = lax.broadcasted_iota(jnp.int32, shape, 0) == lax.broadcasted_iota(jnp.int32, shape, 1)
                block = stage[slot, :, at].astype(jnp.float32)
                stage[slot, :, at] = jnp.where(same, 0.0, block).astype(stage.dtype)

        write(i, slot).start()

    write(rows - 2, (rows - 2) % 2).wait()
    write(rows - 1, (rows - 1) % 2).wait()


def product(left, right, reads, section_count):
    rows, cols, bins = left.shape[0], right.shape[0], left.shape[1]

    def kernel(*refs):
        product_kernel(1.0 / math.sqrt(bins), *refs)

    return pl.pallas_call(
        kernel,
        out_shape=jax.ShapeDtypeStruct((rows, cols), left.dtype),
        in_specs=[pl.BlockSpec(memory_space=pltpu.VMEM)] * 2,
        out_specs=pl.BlockSpec(memory_space=pl.ANY),
        scratch_shapes=[
            pltpu.SMEM((rows // reads, section_count), jnp.int32),
            pltpu.SMEM((cols // reads, section_count), jnp.int32),
            pltpu.VMEM((2, reads, cols), left.dtype),
            pltpu.SemaphoreType.DMA((2,)),
        ],
        compiler_params=pltpu.CompilerParams(vmem_limit_bytes=16 << 20),
        name="product",
    )(left, right)


def shards(weights, tile_pattern):
    left, right = gather(tile_pattern, weights)
    return product(left, right, weights.shape[0], tile_pattern.shape[1])


def solution(mesh):
    return jax.shard_map(
        shards,
        mesh=mesh,
        in_specs=(P(("row", "col"), None), P(("row", "col"), None)),
        out_specs=P("row", "col"),
        check_vma=False,
    )
```

```python
import math

import jax
import jax.numpy as jnp
from jax import lax
from jax.experimental import pallas as pl
from jax.experimental.pallas import tpu as pltpu
from jax.sharding import PartitionSpec as P

MESH = pl.DeviceIdType.MESH
CHUNKS = 4
SLOTS = (
    (
        (0,0,((0,0,0,1,4,6),(0,1,0,5,6),(0,2,0,3,6),(0,3,0,2,4,6))),
        (0,1,((1,0,0,1,2),(1,1,0,1),(1,2,1,2),(1,3,1))),
        (0,2,((2,0,0),(2,1,1),(2,2,0,2),(2,3,1))),
        (0,3,((3,0,0,1),(3,1,0,2),(3,2,0,1),(3,3,0,1))),
        (0,4,((4,0,0),(4,1,0,2),(4,2,0,2),(4,3,0,1,2))),
        (0,5,((5,0,0,1,2),(5,1,0,1),(5,2,0,1),(5,3,0,1,2))),
        (0,6,((6,0,0),(6,1,0,2),(6,2,1),(6,3,0,1))),
        (0,7,((7,0,0),(7,1,0,1,2),(7,2,0),(7,3,0,1,2))),
    ),
    (),
    (),
    (),
    (),
    (),
    (),
    (
        (0,0,((4,1,0,4,6),(3,0,3,6),(1,0,5,6))),
        (0,1,((5,0,0,1),(0,0))),
        (0,2,((1,0,0),(3,0,1))),
        (0,3,((2,0,0,2),(0,0,1,2))),
        (0,4,((7,0,0,2),(5,0))),
        (0,5,((1,0,1),(4,0,0))),
        (0,6,((5,0,0),)),
        (0,7,((6,0,0,2),)),
    ),
    (
        (0,1,((2,1,1,2),)),
        (0,5,((6,2,2),)),
        (0,6,((7,1),)),
        (1,3,((0,0,4,6),)),
        (1,4,((0,1,3,4,6),)),
    ),
    (
        (0,3,((7,1,0,1),)),
        (0,7,((4,3,1),(3,1,0,1))),
        (1,1,((0,2,3,5,6),)),
    ),
    (
        (0,6,((2,2,0,1),)),
    ),
    (
        (0,0,((4,2,0,5,6),)),
        (0,2,((6,1,0),)),
    ),
    (
        (0,0,((3,1,0,3,6),(1,1,4,6))),
        (0,1,((0,1,0),(2,3,1,2),(5,3,0,1))),
        (0,2,((1,1,0),(3,2,1))),
        (0,3,((2,2,0),)),
        (0,4,((7,1,0),(5,1,2))),
        (0,5,((4,1,0),(1,2,1))),
        (0,6,((5,1,0),(7,3,1))),
        (0,7,((6,1,0),)),
        (1,3,((0,3,4,5,6),)),
    ),
    (
        (0,5,((6,3,1),)),
    ),
    (
        (0,0,((4,3,0,1,3,6),)),
        (0,4,((0,3,0),)),
    ),
    (
        (0,3,((7,3,1),)),
        (0,7,((2,0,1,0),)),
        (1,1,((3,0,3,6),)),
        (1,2,((0,0,4,5,6),)),
    ),
    (
        (0,0,((7,0,1,0,4,6),(3,2,5,6),(1,2,1,5,6))),
        (0,1,((0,2,0),)),
        (0,2,((5,0),(3,3,1,2))),
        (0,3,((1,0),)),
        (0,4,((7,2,0,2),(5,2,2))),
        (0,5,((4,2,0),)),
        (0,6,((5,2,0),)),
        (0,7,((6,3,2),)),
        (1,5,((0,1,6),)),
        (1,7,((0,1,4,6),)),
    ),
    (
        (0,1,((3,0,2),)),
        (0,3,((6,0,0),)),
        (0,5,((2,2),)),
        (0,6,((4,3),)),
        (0,7,((0,0,0),)),
        (1,2,((0,2,6),)),
        (1,3,((4,1,4,5,6),)),
        (1,4,((1,0,3,4,6),)),
    ),
    (),
    (),
    (
        (0,1,((6,2,0,1),)),
        (0,5,((2,1,1),)),
        (1,1,((3,1,3,6),)),
        (1,2,((0,3,4,6),)),
    ),
    (
        (0,0,((5,1,1,5,6),(3,3,4,6),(1,3,1,3,6))),
        (0,1,((0,3,0),(3,2,2))),
        (0,2,((0,1,0,2),(0,0))),
        (0,3,((6,1,0),(4,3,1))),
        (0,4,((7,3),(5,3,1))),
        (0,5,((4,3),)),
        (0,6,((5,3),(3,1))),
        (0,7,((5,0),)),
        (1,3,((1,1,4,5,6),)),
        (1,5,((0,2,3,6),)),
    ),
    (
        (0,5,((7,3),)),
        (1,4,((4,2,3,4,6),)),
    ),
    (
        (1,1,((0,0,6),)),
        (1,2,((3,0,3,5,6),)),
        (1,7,((0,3,3,4,6),)),
    ),
    (
        (0,5,((2,3,0,1),)),
        (1,1,((4,3,3,5,6),)),
        (1,2,((4,1,4,6),)),
        (1,6,((0,1,5,6),(0,0,4,3,6))),
    ),
    (
        (0,0,((7,2,1,0,3,6),(2,0,0,3,6),(5,0,1,4,6))),
        (0,1,((4,1),)),
        (0,2,((5,3),(7,1,1))),
        (0,3,((1,1,2),)),
        (0,4,((6,0,0),(1,0,1))),
        (0,5,((7,0,0),)),
        (0,6,((4,0,0,2),)),
        (0,7,((2,2,0),)),
        (1,5,((1,0,5,3,6),)),
        (1,7,((1,0,5,6),)),
    ),
    (
        (0,1,((3,3),)),
        (0,3,((7,0,1),)),
        (0,6,((2,0),)),
        (1,3,((7,0,4,6),)),
        (1,4,((3,2,3,4,6),)),
    ),
    (
        (0,0,((5,2,0,3,6),)),
        (1,2,((3,1,3,5,6),)),
    ),
    (
        (1,1,((0,3,6),)),
    ),
    (
        (0,3,((6,3,1,0),)),
        (0,6,((3,3,0,1),)),
        (0,7,((5,3),)),
        (1,1,((1,3,3,6),)),
        (1,2,((1,1,4,6),)),
        (1,5,((4,2,5,6),)),
        (1,6,((0,2,3,6),)),
    ),
    (
        (0,0,((7,1,4,6),(2,1,1,4,6))),
        (0,1,((4,2,0),)),
        (0,2,((0,2,0,2),(7,3,1))),
        (0,3,((0,1),(1,2,1))),
        (0,4,((3,1,0),(1,2,1))),
        (0,5,((7,1),)),
        (0,6,((4,1,0),)),
        (0,7,((5,1),)),
        (1,3,((3,3,4,5,6),(3,0,6))),
        (1,4,((0,3,3,6),)),
        (1,6,((0,3,6),)),
        (1,7,((4,2,5,4,6),)),
    ),
    (
        (1,4,((1,2,3,4,6),)),
    ),
    (
        (0,5,((3,0,1,0),)),
        (1,1,((4,1,6),)),
        (1,2,((0,1,4,3,6),(4,3,3,6))),
        (1,5,((0,0,4,6),)),
        (1,7,((4,1,3,4,6),(0,0,6))),
    ),
    (
        (0,1,((7,1),)),
        (0,7,((1,0,1),)),
        (1,1,((1,0,3,6),)),
        (1,2,((7,0,4,5,6),)),
        (1,3,((1,0,6),)),
    ),
    (
        (0,0,((2,2,0,5,6),(2,3,1,3,5,6))),
        (0,1,((3,1,0),)),
        (0,2,((6,2),(4,3))),
        (0,4,((6,1,0),(6,3))),
        (0,5,((0,3),)),
        (0,6,((0,1,1,0),(4,2,0))),
        (0,7,((5,2),)),
        (1,5,((3,2,5,6),)),
        (1,6,((3,0,4,3,6),(1,0,6))),
        (1,7,((3,2,5,4,6),)),
    ),
    (
        (1,3,((5,0,4,6),(3,1,6))),
        (1,4,((5,1,3,4,6),)),
        (1,5,((4,3,4,3,6),)),
    ),
    (
        (0,5,((3,2,1,0),)),
        (0,7,((1,1,1,0),)),
        (1,1,((2,0,3,5,6),(7,2,5,6))),
    ),
    (
        (0,3,((1,3,1,2),(5,1,1))),
        (0,5,((3,3,1),)),
        (1,1,((1,1,6),)),
        (1,2,((1,3,3,5,6),)),
    ),
    (
        (0,1,((7,3,1),)),
        (0,2,((4,0,1,0),)),
        (0,3,((0,2),)),
        (0,7,((1,2,1),)),
        (1,2,((3,3,4,5,6),)),
        (1,6,((4,2,5,6),)),
        (1,7,((1,1,3,4,6),)),
    ),
    (
        (0,0,((6,0,0,5,6),(5,3,1,4,6))),
        (0,1,((4,3),)),
        (0,2,((0,3,0),(7,0))),
        (0,4,((2,0,0),(2,1,1))),
        (0,5,((7,2,0),)),
        (0,7,((4,0),)),
        (1,1,((4,2,6),)),
        (1,3,((4,2,6),(7,1,4,5,6))),
        (1,4,((4,1,6),)),
        (1,6,((3,1,4,3,6),)),
        (1,7,((1,2,5,4,6),(0,2,5,3,6))),
    ),
    (
        (0,6,((0,2,1,0),)),
        (1,6,((4,1,4,6),)),
    ),
    (
        (0,6,((2,3,0),(7,0),(1,0))),
        (1,1,((0,1,6),)),
        (1,2,((1,0,6),)),
        (1,3,((0,1,6),)),
        (1,4,((0,0,6),)),
        (1,5,((0,3,6),(1,2,5,6))),
    ),
    (
        (1,2,((5,0,4,5,6),)),
        (1,4,((2,2,3,4,6),)),
        (1,5,((3,0,6),)),
        (1,6,((4,3,6),)),
        (1,7,((3,0,3,6),)),
    ),
    (
        (0,0,((6,1,0,4,5,6),(6,2,2,1,3,6))),
        (0,1,((7,0),)),
        (0,2,((4,2,0),(6,3,1))),
        (0,4,((0,0,0),(2,3))),
        (0,5,((0,1),(6,0))),
        (0,7,((3,3),)),
        (1,1,((5,2,3,5,6),(3,2,6))),
        (1,3,((4,3,6),(3,2,4,6))),
        (1,4,((4,3,4,6),)),
        (1,7,((5,1,6),)),
    ),
    (
        (1,3,((2,1,4,5,6),)),
        (1,5,((2,0,4,3,6),(7,2,4,3,6))),
        (1,6,((7,0,3,6),)),
    ),
    (
        (0,6,((1,1),)),
        (1,7,((3,3,6),)),
    ),
    (
        (0,1,((4,0,1),)),
        (0,3,((4,0),(5,0),(7,2,1))),
        (1,1,((7,0,5,6),)),
        (1,2,((2,0,3,6),(4,2,6))),
    ),
    (
        (0,7,((2,1,1),)),
        (1,1,((2,3,3,6),)),
        (1,2,((7,1,4,6),)),
        (1,4,((2,3,3,6),)),
        (1,5,((5,1,3,6),)),
        (1,6,((3,2,6),)),
    ),
    (
        (0,0,((6,3,3,5,6),(7,3,3,4,5,6))),
        (0,2,((3,1),(1,2))),
        (0,4,((2,2),(3,0,1))),
        (0,5,((3,1),(0,2))),
        (0,6,((3,0),)),
        (0,7,((4,1,2),(1,3,1,0))),
        (1,3,((5,3,4,5,6),)),
        (1,4,((1,1,6),(0,2,6))),
        (1,5,((3,1,4,6),)),
        (1,7,((3,1,6),)),
    ),
    (
        (1,1,((1,2,6),)),
        (1,3,((1,3,6),)),
        (1,5,((4,1,6),)),
        (1,6,((1,3,4,3,6),)),
    ),
    (
        (0,1,((2,0),(7,2))),
        (0,6,((1,2),)),
        (1,1,((3,3,6),)),
        (1,2,((5,2,3,6),)),
        (1,3,((0,2,6),)),
        (1,7,((7,1,3,4,6),(2,2,5,6))),
    ),
    (
        (0,1,((6,3),)),
        (0,3,((0,3,2),)),
        (1,4,((6,0,3,4,6),)),
        (1,5,((5,2,4,6),)),
        (1,6,((1,2,5,6),)),
    ),
    (
        (0,4,((1,1,0),)),
        (0,5,((6,1),)),
        (1,1,((6,2,3,5,6),)),
        (1,3,((1,2,6),)),
        (1,4,((3,0,6),)),
        (1,5,((2,2,5,3,6),)),
        (1,6,((2,0,3,6),(7,2,5,6))),
        (1,7,((7,0,3,6),)),
    ),
    (
        (0,3,((2,1),)),
        (0,4,((3,2,1),)),
        (0,6,((3,2),)),
        (1,2,((2,1,4,6),)),
        (1,3,((6,1,4,6),(2,0,6))),
        (1,4,((2,0,6),(7,2,4,6))),
        (1,6,((1,1,4,6),(3,3,4,6))),
        (1,7,((4,3,6),)),
    ),
    (
        (0,0,((4,0,3,4,5,6),)),
        (0,7,((0,1,0),(4,2))),
        (1,7,((2,1,3,4,6),)),
    ),
    (
        (0,2,((1,3),(5,1,1))),
        (0,3,((4,2),)),
        (1,1,((5,0,5,6),)),
        (1,2,((2,3,3,5,6),(3,2,6))),
    ),
    (
        (0,4,((3,3),)),
        (0,6,((7,2),(2,1))),
        (0,7,((3,0),)),
        (1,4,((6,1,3,4,6),)),
        (1,5,((7,0,6),(2,3,6))),
    ),
    (
        (0,1,((5,2,0),)),
        (0,3,((2,3),)),
        (0,5,((2,0),)),
        (1,1,((6,3,3,6),)),
        (1,3,((7,3,6),)),
        (1,4,((3,1,6),)),
        (1,5,((1,3,6),)),
    ),
    (
        (0,4,((1,3,0),)),
        (1,3,((5,2,5,6),)),
        (1,6,((5,1,5,6),(5,0,3,6))),
        (1,7,((1,3,3,6),)),
    ),
    (
        (0,4,((6,2,1),)),
        (0,6,((1,3),)),
        (1,1,((7,1,6),)),
        (1,3,((2,2,4,6),)),
        (1,6,((7,1,4,6),)),
        (1,7,((5,3,3,4,6),)),
    ),
    (
        (0,3,((4,1,1),)),
        (1,1,((2,2,6),)),
        (1,2,((6,2,3,6),(5,3,4,6))),
        (1,4,((7,1,6),)),
        (1,7,((2,0,6),)),
    ),
    (
        (0,1,((2,2),)),
        (0,2,((7,2),)),
        (0,5,((0,0,0),)),
        (0,7,((0,3,1),)),
        (1,1,((7,3,3,6),)),
        (1,2,((7,2,6),)),
        (1,5,((6,0,5,3,6),(6,2,4,3,6))),
        (1,7,((6,0,5,6),)),
    ),
    (
        (0,1,((5,1),)),
        (0,3,((5,3),)),
        (0,7,((3,2),(0,2,0))),
        (1,2,((1,2,6),)),
        (1,3,((4,0,5,6),(2,3,6))),
        (1,4,((5,2,6),(6,3,3,4,6))),
        (1,5,((3,3,4,6),)),
        (1,7,((7,2,5,6),)),
    ),
    (
        (0,4,((0,1),)),
        (1,4,((7,0,6),)),
        (1,5,((1,1,6),)),
        (1,6,((2,2,6),)),
    ),
    (
        (0,2,((5,2,0),)),
        (1,1,((2,1,5,6),)),
        (1,2,((6,3,3,6),)),
        (1,6,((2,1,6),)),
    ),
    (
        (0,7,((2,3),)),
        (1,2,((6,1,5,6),)),
        (1,5,((6,1,5,6),)),
        (1,6,((2,3,3,6),)),
    ),
    (
        (0,1,((6,0,0),)),
        (0,3,((6,2),)),
        (0,5,((1,1),)),
        (1,1,((4,0,3,5,6),)),
        (1,5,((5,0,4,6),)),
        (1,7,((5,2,4,6),(6,1,6),(5,0,6))),
    ),
    (
        (1,3,((6,2,5,6),)),
        (1,4,((7,3,3,4,6),)),
    ),
    (
        (0,2,((4,1),)),
        (0,7,((6,2),)),
        (1,1,((5,3,6),)),
        (1,2,((5,1,4,3,6),)),
        (1,3,((6,0,6),)),
        (1,4,((2,1,6),)),
    ),
    (
        (0,6,((0,0),(0,3))),
        (1,1,((6,0,3,6),)),
        (1,2,((7,3,5,6),(2,2,6))),
        (1,3,((7,2,6),)),
        (1,6,((5,3,4,6),)),
    ),
    (
        (0,1,((6,1),)),
        (0,5,((1,3),)),
        (1,5,((7,1,6),(6,3,3,6))),
        (1,6,((6,0,6),(6,2,6))),
        (1,7,((4,0,4,6),)),
    ),
    (
        (0,4,((0,2),)),
        (1,4,((3,3,6),(4,0,6))),
    ),
    (
        (0,3,((5,2),)),
        (1,3,((6,3,6),)),
        (1,4,((6,2,6),(1,3,6))),
        (1,5,((2,1,6),)),
        (1,7,((6,3,6),)),
    ),
    (
        (0,2,((6,0),)),
        (1,1,((6,1,6),)),
        (1,2,((4,0,6),)),
        (1,6,((6,1,6),)),
        (1,7,((2,3,6),)),
    ),
    (
        (1,5,((7,3,6),)),
        (1,6,((5,2,6),)),
    ),
    (
        (1,7,((6,2,6),)),
    ),
    (
        (1,1,((5,1,6),)),
        (1,4,((5,3,6),(5,0,6))),
        (1,5,((4,0,6),(5,3,6))),
        (1,7,((7,3,6),)),
    ),
    (
        (1,3,((5,1,6),)),
        (1,6,((7,3,6),)),
    ),
    (
        (1,2,((6,0,6),)),
        (1,6,((6,3,6),(4,0,6))),
    ),
    (),
    (),
    (),
    (),
    (),
    (),
    (),
    (),
)
ROW_ORDER = ((0,3,1,2,5,6,7,4),(1,0,3,4,7,2,5,6),(2,0,3,1,7,5,4,6),(3,1,7,0,2,4,6,5),(4,7,5,2,3,1,6,0),(5,4,7,3,6,2,0,1),(6,5,4,3,7,2,1,0),(7,5,1,4,3,0,2,6))
COL_ORDER = ((0,3,1,2,5,6,7,4),(0,1,3,7,2,4,6,5),(0,3,1,5,7,2,4,6),(3,0,1,4,2,7,6,5),(0,7,2,3,4,6,1,5),(0,3,1,6,2,7,4,5),(0,1,3,2,5,7,6,4),(0,3,1,5,4,2,6,7))
READY = (51, 69, 70, 73, 76, 80, 80, 81)
STEPS = ((0,0),(1,0),(2,0),(3,0),(4,0),(5,0),(6,0),(0,1),(1,1),(2,1),(3,1),(4,1),(5,1),(6,1),(0,2),(1,2),(2,2),(3,2),(4,2),(5,2),(6,2),(7,0),(7,1),(7,2))
FIRST_STEP = 63
XP, XM, ZH, YP, YM, ZL, CORE = range(7)


def place():
    row, col = lax.axis_index("row"), lax.axis_index("col")
    return col // 2, lax.rem(col, 2), lax.rem(row // 2, 4), row // 8, lax.rem(row, 2)


def device(x, zh, y, zl, core):
    return (zl * 8 + y * 2 + core, x * 2 + zh)


def neighbours(x, zh, y, zl, core):
    def turn(a, by):
        return lax.rem(a + by, 4)

    return {
        XP: device(turn(x, 1), zh, y, zl, core),
        XM: device(turn(x, 3), zh, y, zl, core),
        ZH: device(x, 1 - zh, y, zl, core),
        YP: device(x, zh, turn(y, 1), zl, core),
        YM: device(x, zh, turn(y, 3), zl, core),
        ZL: device(x, zh, y, 1 - zl, core),
        CORE: device(x, zh, y, zl, 1 - core),
    }


def flip(a, b):
    return a + b - 2 * a * b


def pick(values, at):
    out = jnp.int32(values[0])
    for n, value in enumerate(values[1:], 1):
        out = jnp.where(at == n, jnp.int32(value), out)
    return out


def packed(entries, bits):
    out = 0
    for n, entry in enumerate(entries):
        out += entry << (bits * n)
    return out


def digit(code, at, bits):
    return lax.rem(lax.shift_right_logical(code, bits * at), 1 << bits)


class Place:
    def __init__(self):
        self.coordinates = x, zh, y, zl, core = place()
        self.core = core
        self.row_root = (2 * zl + y // 2, lax.rem(y, 2))
        self.col_root = (2 * lax.rem(x, 2) + zh, x // 2)
        self.row_place = lax.rem(x - self.row_root[0] + 4, 4) + 4 * flip(zh, self.row_root[1])
        self.col_place = lax.rem(y - self.col_root[0] + 4, 4) + 4 * flip(zl, self.col_root[1])
        self.row_code = pick([packed(order, 3) for order in ROW_ORDER], self.row_place)
        self.col_code = pick([packed(order, 3) for order in COL_ORDER], self.col_place)

    def row_shard(self, source):
        return lax.rem(self.row_root[0] + lax.rem(source, 4), 4) * 2 + flip(self.row_root[1], source // 4)

    def col_shard(self, source):
        return lax.rem(self.coordinates[0] + lax.rem(source, 4), 4) * 2 + flip(self.coordinates[1], source // 4)

    def row_ranked(self, rank):
        return self.row_shard(digit(self.row_code, rank, 3))

    def col_ranked(self, rank):
        return self.col_shard(digit(self.col_code, rank, 3))


def dot(lhs, rhs):
    return lax.dot_general(lhs, rhs, (((1,), (1,)), ((), ())), preferred_element_type=jnp.float32)


def clear_diagonal(block):
    same = lax.broadcasted_iota(jnp.int32, block.shape, 0) == lax.broadcasted_iota(jnp.int32, block.shape, 1)
    return jnp.where(same, 0.0, block.astype(jnp.float32)).astype(block.dtype)


def gather_kernel(
    scale, pattern_ref, weights_ref, left, right, blocks, send_sems, row_sems, col_sems, core_sems, local_sems
):
    reads, bins = weights_ref.shape
    section_count = pattern_ref.shape[1]
    bin_tile = bins // section_count
    piece = reads // CHUNKS
    x, zh, y, zl, core = place()
    near = neighbours(x, zh, y, zl, core)
    barrier = pltpu.get_barrier_semaphore()
    for target in near.values():
        pl.semaphore_signal(barrier, inc=1, device_id=target, device_id_type=MESH)
    own = pl.multiple_of((x * 2 + zh) * reads, reads)
    for section in range(section_count):
        part = pl.ds(section * bin_tile, bin_tile)
        keep = pattern_ref[0, section].astype(jnp.float32)
        left[pl.ds(own, reads), part] = (weights_ref[:, part].astype(jnp.float32) * keep).astype(left.dtype)
    pl.semaphore_wait(barrier, len(near))

    here = Place()
    row_place, col_place = here.row_place, here.col_place
    row_source = [here.row_shard(s) for s in range(8)]
    col_source = [here.col_shard(s) for s in range(8)]
    row_tile = [pl.multiple_of(a * reads, reads) for a in row_source]
    col_tile = [pl.multiple_of((core * 8 + a) * reads, reads) for a in col_source]

    def in_left(s, c):
        return left.at[pl.ds(row_tile[s] + c * piece, piece)]

    def in_right(s, c):
        return right.at[pl.ds(col_tile[s] + c * piece, piece)]

    def copy(src, dst, way, recv_sem):
        return pltpu.make_async_remote_copy(
            src_ref=src, dst_ref=dst, send_sem=send_sems.at[way], recv_sem=recv_sem, device_id=near[way], device_id_type=MESH
        )

    def handle(kind, role, s, c, ways):
        row_sem = row_sems.at[row_source[s], c]
        col_sem = col_sems.at[col_source[s], c]
        if kind == 0:
            src = in_left(s, c)
            if s != role:
                copy(src, src, XP, row_sem).wait_recv()
        else:
            src = in_right(s, c)
            copy(src, src, YP, col_sem).wait_recv()
        for way in ways:
            if way <= ZH:
                copy(src, src, way, row_sem).start()
            elif way <= ZL:
                copy(src, in_right(s, c), way, col_sem).start()
            else:
                copy(src, in_right(s, c), way, core_sems.at[col_source[s]]).start()
        if kind == 0 and role == 0:
            pltpu.make_async_copy(src, in_right(s, c), local_sems.at[col_source[s]]).start()

    def shard_ready(rank):
        shard = here.col_ranked(rank)
        block = right.at[pl.ds(pl.multiple_of(shard * reads, reads), reads)]
        copy(block, block, CORE, core_sems.at[shard]).wait_recv()

        @pl.when(col_place == 0)
        def _():
            pltpu.make_async_copy(block, block, local_sems.at[shard]).wait()

    first_row = lax.axis_index("row") * 8
    first_col = lax.axis_index("col") * 16

    def multiply(step):
        per = 5
        codes = [packed([a * 8 + b for a, b in STEPS[n : n + per]], 6) for n in range(0, len(STEPS), per)]
        pair = digit(pick(codes, step // per), lax.rem(step, per), 6)
        i, shard = here.row_ranked(pair // 8), here.col_ranked(lax.rem(pair, 8))
        rows = pl.ds(pl.multiple_of(i * reads, reads), reads)
        for half in range(2):
            j = half * 8 + shard
            tile = pl.ds(pl.multiple_of(j * reads, reads), reads)
            blocks[j, rows, :] = (dot(left[rows, :], right[tile, :]) * scale).astype(blocks.dtype)
        for half in range(2):
            j = half * 8 + shard

            @pl.when(first_row + i == first_col + j)
            def _(j=j):
                blocks[j, rows, :] = clear_diagonal(blocks[j, rows, :])

    sent = {}

    def run_slot(slot):
        for kind, role, entries in SLOTS[slot]:
            for entry in entries:
                for way in entry[2:]:
                    at = (0 if way <= ZH else 1, role, way)
                    sent[at] = sent.get(at, 0) + 1

            @pl.when((row_place if kind == 0 else col_place) == role)
            def _(kind=kind, role=role, entries=entries):
                for entry in entries:
                    handle(kind, role, entry[0], entry[1], entry[2:])

        for rank, at in enumerate(READY):
            if at == slot:
                shard_ready(rank)

    def dispatch(slot, low, high):
        if high - low == 1:
            run_slot(low)
            return
        middle = (low + high) // 2

        @pl.when(slot < middle)
        def _():
            dispatch(slot, low, middle)

        @pl.when(slot >= middle)
        def _():
            dispatch(slot, middle, high)

    @pl.loop(0, len(SLOTS))
    def _(slot):
        dispatch(slot, 0, len(SLOTS))

        @pl.when(jnp.logical_and(slot >= FIRST_STEP, slot < FIRST_STEP + len(STEPS)))
        def _():
            multiply(slot - FIRST_STEP)

    def held(count):
        return right.at[pl.ds(0, count * piece)]

    for (kind, role, way), count in sorted(sent.items()):

        @pl.when((row_place if kind == 0 else col_place) == role)
        def _(way=way, count=count):
            copy(held(count), held(count), way, core_sems.at[0]).wait_send()


def gather(tile_pattern, weights):
    reads, bins = weights.shape

    def kernel(*refs):
        gather_kernel(1.0 / math.sqrt(bins), *refs)

    return pl.pallas_call(
        kernel,
        out_shape=(
            pltpu.VMEM((8 * reads, bins), weights.dtype),
            pltpu.VMEM((16 * reads, bins), weights.dtype),
            pltpu.VMEM((16, 8 * reads, reads), weights.dtype),
        ),
        in_specs=[pl.BlockSpec(memory_space=pltpu.SMEM), pl.BlockSpec(memory_space=pltpu.VMEM)],
        out_specs=(pl.BlockSpec(memory_space=pltpu.VMEM),) * 3,
        scratch_shapes=[
            pltpu.SemaphoreType.DMA((7,)),
            pltpu.SemaphoreType.DMA((8, CHUNKS)),
            pltpu.SemaphoreType.DMA((8, CHUNKS)),
            pltpu.SemaphoreType.DMA((8,)),
            pltpu.SemaphoreType.DMA((8,)),
        ],
        compiler_params=pltpu.CompilerParams(collective_id=0, has_side_effects=True, vmem_limit_bytes=8 << 20),
        name="gather",
    )(tile_pattern, weights)


def finish_kernel(scale, done, left, right, blocks, out, stage, sems):
    here = Place()
    tile = blocks.shape[2]
    rows = left.shape[0] // tile
    first_row = lax.axis_index("row") * rows
    first_col = lax.axis_index("col") * 16

    def panel(n):
        return lax.rem(n, 2) * 8 + here.col_ranked(n // 2)

    def write(n, src):
        return pltpu.make_async_copy(src, out.at[:, pl.ds(pl.multiple_of(panel(n) * tile, tile), tile)], sems.at[n])

    for n in range(done):
        write(n, blocks.at[panel(n)]).start()

    @pl.loop(0, 16 - done)
    def _(n):
        j = panel(done + n)
        at = pl.ds(pl.multiple_of(j * tile, tile), tile)
        stage[n] = (dot(left[...], right[at, :]) * scale).astype(stage.dtype)
        i = first_col + j - first_row

        @pl.when(jnp.logical_and(i >= 0, i < rows))
        def _():
            part = pl.ds(pl.multiple_of(i * tile, tile), tile)
            stage[n, part, :] = clear_diagonal(stage[n, part, :])

        write(done + n, stage.at[n]).start()

    for n in range(16):
        write(n, blocks.at[n]).wait()


def finish(left, right, blocks):
    rows, bins = left.shape
    count, _, tile = blocks.shape
    done = 2 * (1 + max(b for _, b in STEPS))

    def kernel(*refs):
        finish_kernel(1.0 / math.sqrt(bins), done, *refs)

    return pl.pallas_call(
        kernel,
        out_shape=jax.ShapeDtypeStruct((rows, count * tile), left.dtype),
        in_specs=[pl.BlockSpec(memory_space=pltpu.VMEM)] * 3,
        out_specs=pl.BlockSpec(memory_space=pl.ANY),
        scratch_shapes=[pltpu.VMEM((max(16 - done, 1), rows, tile), left.dtype), pltpu.SemaphoreType.DMA((count,))],
        compiler_params=pltpu.CompilerParams(vmem_limit_bytes=16 << 20),
        name="finish",
    )(left, right, blocks)


def shards(weights, tile_pattern):
    return finish(*gather(tile_pattern, weights))


def solution(mesh):
    return jax.shard_map(
        shards,
        mesh=mesh,
        in_specs=(P(("row", "col"), None), P(("row", "col"), None)),
        out_specs=P("row", "col"),
        check_vma=False,
    )
```

```python
import math

import jax
import jax.numpy as jnp
from jax import lax
from jax.experimental import pallas as pl
from jax.experimental.pallas import tpu as pltpu
from jax.sharding import PartitionSpec as P

MESH = pl.DeviceIdType.MESH
CHUNKS = 8
UNITS = 2
SLOTS = (
    (
        (0,0,((0,0,1,5),(0,1,0,1,4),(0,2,1,4),(0,3,0,3,6),(0,4,0,1,4),(0,5,0,3),(0,6,1,5),(0,7,0,1,5,6))),
        (0,1,((1,0,0,1),(1,1,0,1,2),(1,2,0,1,2),(1,3,0),(1,4,0,1),(1,5,0,2),(1,6,0,1),(1,7,0,2))),
        (0,2,((2,0,1,2),(2,1,0,2),(2,2,1),(2,3,0,1,2),(2,4,0,2),(2,5,0,1,2),(2,6,1),(2,7,2))),
        (0,3,((3,0,0,2),(3,1,0,1,2),(3,2,2),(3,3,1),(3,4,1),(3,5,0),(3,6,0,2),(3,7,0,1,2))),
        (0,4,((4,0,0,2),(4,1,0,2),(4,2,0,1),(4,3,0,1),(4,4,1,2),(4,5,0,1),(4,6,0,1,2),(4,7,0,1,2))),
        (0,5,((5,0,1,2),(5,1,1),(5,2,0,1),(5,3,0,2),(5,4,0,1),(5,5,2),(5,6,1,2),(5,7,1,2))),
        (0,6,((6,0,0),(6,1,0,2),(6,2,1,2),(6,3,0,2),(6,4,1,2),(6,5,0),(6,6,0,2),(6,7,1,2))),
        (0,7,((7,0,1),(7,1,0,1),(7,2,0,1,2),(7,3,0,1),(7,4,2),(7,5,1),(7,6,1),(7,7,0,1,2))),
    ),
    (),
    (),
    (),
    (),
    (
        (0,0,((3,0,0,4),(1,0,1,3))),
        (0,1,((2,0),(0,1))),
        (0,2,((1,0,2),(3,1,2))),
        (0,3,((0,0,1),(2,1,0))),
        (0,4,((5,0,1),(7,1,0,2))),
        (0,5,((4,0,0,2),)),
        (0,6,((7,0,1,2),)),
        (0,7,((6,0,0),)),
        (1,4,((0,0,3),)),
    ),
    (
        (0,0,((4,0,1,3,5),)),
        (0,1,((5,0,0,1),)),
        (0,5,((6,2,1),)),
        (0,6,((5,2),(2,0,1))),
        (0,7,((4,2,1,2),(3,0,0))),
        (1,1,((0,3,3),)),
        (1,3,((0,1,4),)),
    ),
    (
        (0,0,((3,1,4),(1,1,5))),
        (0,1,((2,2,1,2),)),
        (0,2,((6,1,0),(1,1,0))),
        (0,3,((7,2,1),(0,1,1))),
        (0,4,((5,1,1,2),)),
        (0,5,((1,1,0),(4,1,0))),
        (0,6,((7,1),)),
        (0,7,((6,1,0),)),
        (1,4,((0,6,3,4),)),
    ),
    (
        (0,1,((0,3,0),)),
        (0,2,((3,3,1,2),)),
        (0,3,((2,3,0),)),
        (0,4,((7,2,0),)),
        (0,5,((6,4,1,2),)),
        (0,6,((5,3,0),)),
        (0,7,((4,3,2),)),
        (1,3,((0,2,4,5),)),
    ),
    (
        (0,0,((4,1,1,3),)),
        (0,1,((5,3,0),)),
        (0,2,((6,2,1),)),
        (0,3,((7,4,0,1),)),
        (0,5,((1,2,0),)),
        (0,6,((2,1,1),)),
        (0,7,((3,1),)),
        (1,1,((0,5,3,5),)),
    ),
    (
        (0,0,((3,5,0,5),(1,2,1,5))),
        (0,1,((2,3),(0,4))),
        (0,2,((1,2),(3,4,1,2))),
        (0,3,((0,2,1),(2,4,0))),
        (0,4,((5,2,1),(7,3,0))),
        (0,5,((4,2),(6,7,1))),
        (0,6,((7,2),(5,4))),
        (0,7,((6,3,0),(4,4,1))),
        (1,3,((0,4,4),)),
        (1,4,((0,7,3,4),)),
    ),
    (
        (0,0,((4,4,1,3),)),
        (0,1,((5,5,0),)),
        (0,2,((6,3,1),)),
        (0,3,((7,7,0,1),)),
        (0,5,((1,5,1),)),
        (0,6,((2,3,1),)),
        (0,7,((3,2,0,1),)),
        (1,1,((1,0,3),)),
        (1,2,((0,1,4,5),)),
        (1,5,((0,0,5,3),)),
    ),
    (
        (0,0,((3,6,5),(1,4,1,4))),
        (0,1,((2,5),(0,5,0))),
        (0,2,((1,3,0,2),(3,7,1))),
        (0,3,((0,4,1,2),(2,5,0))),
        (0,4,((5,4,2),(7,7,0))),
        (0,5,((4,3,0,2),(7,0,1))),
        (0,6,((7,3,2),(4,0,0))),
        (0,7,((6,5,0,2),(4,5))),
        (1,2,((0,3,3,5),)),
        (1,3,((3,0,4,5),)),
        (1,4,((4,0,3,4),)),
    ),
    (
        (0,0,((4,6,0,4),)),
        (0,1,((5,6,0,1),)),
        (0,2,((6,4),)),
        (0,5,((1,7,1),)),
        (0,6,((2,4,0),)),
        (0,7,((3,6,0,1),)),
        (1,1,((4,0,3),)),
        (1,5,((0,6),)),
        (1,7,((0,6,5,4),)),
    ),
    (
        (0,0,((3,7,5),(1,6,3))),
        (0,1,((2,6,1,2),(0,7))),
        (0,2,((1,4,2),(0,0,1,2))),
        (0,3,((4,2,0,1),(0,6,1,2),(6,1,0))),
        (0,4,((5,6,1),(6,0,0,2))),
        (0,5,((4,5,0,2),)),
        (0,6,((7,5,2),)),
        (0,7,((6,6,0),)),
        (1,2,((0,2,4),(0,5,3))),
        (1,4,((1,1,3,4),)),
    ),
    (
        (0,0,((4,7,0,1,3),)),
        (0,1,((5,7,0,1),)),
        (0,5,((2,0,1),)),
        (0,6,((1,1,0),(2,5,0))),
        (0,7,((4,6,1,2),(3,7,1))),
        (1,3,((3,1,4,5),)),
    ),
    (
        (0,0,((2,1,0,4),(5,0,1,4))),
        (0,1,((3,3,1,2),)),
        (0,2,((6,6,0),(1,5,0))),
        (0,3,((4,3,1),(0,7,1,2))),
        (0,4,((5,7,1),)),
        (0,5,((2,2,0,1),(4,6))),
        (0,6,((7,6,1,2),)),
        (0,7,((5,3,0),)),
        (1,1,((4,1,3),)),
        (1,2,((0,4,4,5),)),
        (1,5,((0,7,5,3),)),
        (1,7,((0,7),)),
    ),
    (
        (0,1,((3,0,0),)),
        (0,2,((7,2,1),)),
        (0,3,((1,1),)),
        (0,4,((3,0,0),)),
        (0,5,((2,1,1),)),
        (0,6,((4,1,0),)),
        (0,7,((4,7),)),
        (1,1,((0,1),)),
        (1,2,((1,0,3,5),)),
        (1,4,((3,5,3,4),)),
        (1,6,((0,0,3),(0,1,4,3))),
    ),
    (
        (0,0,((7,1,4),)),
        (0,1,((4,0,0),)),
        (0,2,((6,7,0,1),)),
        (0,6,((2,7,0),)),
        (1,1,((4,4,3,5),)),
        (1,2,((3,0,4),)),
        (1,3,((1,4,4,5),(0,3))),
        (1,5,((4,0),)),
        (1,7,((4,0,4),)),
    ),
    (
        (0,0,((2,3,4,5),(2,2,1,3))),
        (0,1,((6,2,1),(3,5,0,2))),
        (0,2,((1,6,0,2),(0,1,2))),
        (0,3,((1,0),(1,3,0))),
        (0,4,((6,2,1),(6,1,0))),
        (0,5,((4,7,0),(2,3,1))),
        (0,6,((7,7),(1,2,0))),
        (0,7,((4,0),(5,0))),
        (1,2,((4,0,3),)),
        (1,4,((1,2,3,4),)),
        (1,6,((0,6,5),)),
    ),
    (
        (0,0,((5,1,0,1,5),)),
        (0,1,((6,4,1),)),
        (0,2,((7,0,0,1),)),
        (0,3,((6,5,1,0),)),
        (0,6,((1,0,1,0),)),
        (0,7,((0,4,0),)),
        (1,1,((0,0,3),(0,2,6),(1,6,3,5))),
        (1,2,((3,1,4),)),
        (1,3,((4,6,4),(0,5))),
        (1,5,((0,5,4,3),(1,1,5))),
        (1,7,((0,2,3,4),(1,1,4))),
    ),
    (
        (0,0,((7,4,0,3),(5,6,1,5))),
        (0,1,((3,4,1),(4,6,0))),
        (0,2,((1,7),(7,4))),
        (0,3,((4,0),(6,6,0))),
        (0,4,((6,4,1),(6,3,0))),
        (0,5,((7,1,2),)),
        (0,6,((4,2),(4,3))),
        (0,7,((2,4,0),(5,1,1))),
        (1,4,((3,6,3,4),)),
        (1,6,((0,3,4,3),)),
    ),
    (
        (0,5,((2,6,0,1),(7,6,1))),
        (0,6,((3,1,1),)),
        (1,1,((0,4),(4,7,3,5))),
        (1,2,((4,1,3,5),)),
        (1,3,((2,1,4),(0,6))),
        (1,6,((0,7,5),)),
        (1,7,((0,0),)),
    ),
    (
        (0,0,((2,4,0,5),(2,6,1,3,4))),
        (0,1,((6,3,1),(4,7))),
        (0,2,((5,0,2),(7,3,0,1),(0,2,1,2))),
        (0,3,((4,1,1),(4,6),(1,5,2))),
        (0,4,((6,7,1),(3,2,2,0))),
        (0,5,((7,2),)),
        (0,6,((4,4,1),)),
        (0,7,((1,1,0),(0,6,0,1))),
        (1,2,((1,4),)),
        (1,3,((1,0),)),
        (1,4,((3,7,3,4),)),
        (1,5,((3,5,5),(0,1))),
        (1,7,((3,5,5,4),)),
    ),
    (
        (0,0,((5,4,0,1,4,5),)),
        (0,1,((4,3,1),)),
        (0,5,((3,3,1),)),
        (0,6,((4,5),(3,3))),
        (0,7,((5,2,2),)),
        (1,2,((4,4,3),)),
        (1,6,((4,0),)),
        (1,7,((3,0,3,4),)),
    ),
    (
        (0,0,((7,7,0,3),(5,7,4))),
        (0,1,((3,7),)),
        (0,2,((0,3,0,2),)),
        (0,3,((1,2),)),
        (0,4,((1,5,2),)),
        (0,5,((7,3),(1,0))),
        (0,6,((3,2,2),)),
        (0,7,((2,5,0),(0,7,1))),
        (1,1,((2,2,5),(3,0))),
        (1,3,((5,0,4),(4,0))),
        (1,5,((1,2,3),)),
        (1,7,((0,1,3),(1,2,5))),
    ),
    (
        (0,1,((2,1),)),
        (0,2,((7,7),)),
        (0,3,((6,7),)),
        (0,4,((6,5,0),)),
        (0,6,((2,2,0),)),
        (0,7,((5,6,1),)),
        (1,2,((0,6,4),(4,6,5))),
        (1,4,((2,3,4),(0,2,3),(0,5))),
        (1,6,((0,5,3),(0,2,6))),
    ),
    (
        (0,1,((4,5,1,0),)),
        (0,2,((7,5,0,1),)),
        (0,6,((3,4,1),)),
        (1,1,((3,1),(7,4,3,5))),
        (1,2,((0,0,3,6),)),
        (1,3,((7,1,4,5),)),
        (1,5,((4,4,3),(3,6,3),(0,3,4))),
        (1,6,((0,4,4,3,6),)),
        (1,7,((3,6),(0,3,6))),
    ),
    (
        (0,0,((2,5,5),(3,3,3),(6,0,1,0,5))),
        (0,1,((0,0,2),(5,1))),
        (0,2,((5,3,0),(0,4))),
        (0,3,((4,4,1),(1,6))),
        (0,4,((7,0),(3,6))),
        (0,5,((7,7),(3,1,2,1))),
        (0,6,((3,6,2,1),(4,7))),
        (0,7,((4,1),(5,7))),
        (1,1,((0,7),)),
        (1,2,((2,1,4,5),(0,7,3,6))),
        (1,3,((4,1),)),
        (1,4,((5,1,3,4),)),
    ),
    (
        (0,2,((7,6,0,1),)),
        (0,5,((3,5,1,0),)),
        (0,6,((1,3,1,0),)),
        (1,1,((2,6,3),)),
        (1,2,((1,6,3),)),
        (1,3,((2,3,4),)),
        (1,5,((1,6,4,3),)),
        (1,6,((1,1,5),)),
        (1,7,((3,1,3,4),)),
    ),
    (
        (0,0,((4,2,3,5),(6,2,4))),
        (0,1,((7,2,1),(7,4,2))),
        (0,2,((5,5,2,0),(4,2,1))),
        (0,3,((1,4),(7,0,0))),
        (0,4,((1,7,1),(6,6,0))),
        (0,5,((6,0),(4,4))),
        (0,6,((4,6),(2,6,0))),
        (0,7,((2,7,2,0),(6,2,2))),
        (1,1,((1,1),)),
        (1,3,((3,5,4),(4,4))),
        (1,4,((5,6,3,4),)),
        (1,5,((3,7,5),)),
        (1,6,((1,0,4,3),)),
        (1,7,((3,7,5,4),)),
    ),
    (
        (0,6,((1,4,1,0),)),
        (1,1,((7,7,3,5),)),
        (1,2,((5,0,4,5),(4,7,3))),
        (1,3,((2,6,5),)),
        (1,4,((3,0),)),
        (1,6,((3,5),(1,2,5))),
        (1,7,((1,4,3,4),)),
    ),
    (
        (0,0,((6,1,0,3),(6,4,1,5))),
        (0,1,((6,7,1),(2,4))),
        (0,2,((0,5,0,2),(0,6,1))),
        (0,3,((4,7,1),(7,3))),
        (0,4,((2,0,2,1),(5,3))),
        (0,5,((3,0),(3,4,1))),
        (0,6,((3,7,1),)),
        (0,7,((1,2,0),)),
        (1,1,((0,6,6),)),
        (1,4,((2,4,3,4),)),
        (1,5,((4,7,4,3),(0,2,6))),
        (1,7,((0,5),(2,3,4))),
    ),
    (
        (0,1,((7,1,0),)),
        (0,3,((5,2,1,0),)),
        (0,6,((0,0,0),)),
        (0,7,((6,4),)),
        (1,1,((3,5),)),
        (1,2,((7,1,4,5),)),
        (1,3,((0,0,6),)),
        (1,4,((0,1),(0,3,6))),
        (1,5,((0,4,4,6),)),
        (1,6,((4,1,4,3),(3,0,4),(4,4,3))),
    ),
    (
        (0,0,((1,3,3,6),(3,4,4,6))),
        (0,1,((7,0),)),
        (0,2,((5,6),)),
        (0,3,((5,0),)),
        (0,4,((2,2),)),
        (0,5,((6,1),(3,6,2))),
        (0,6,((5,1),)),
        (0,7,((1,5,1),(1,0,0))),
        (1,1,((3,3,3,5),)),
        (1,2,((7,4),)),
        (1,3,((5,4,4),(1,2))),
        (1,7,((0,4,6),)),
    ),
    (
        (0,1,((5,4),)),
        (0,2,((4,3),)),
        (0,3,((0,3,2),)),
        (0,4,((0,4,0),)),
        (0,7,((6,7),)),
        (1,1,((2,1),)),
        (1,4,((5,4,4),(3,1,3))),
        (1,5,((5,1,5),)),
        (1,6,((3,1),)),
        (1,7,((5,1,4),)),
    ),
    (
        (0,0,((3,2,0,4,6),)),
        (0,2,((3,2),)),
        (0,6,((3,5),(1,6,1,0))),
        (1,1,((4,2,3),)),
        (1,2,((2,3,4),(1,1,3),(2,6))),
        (1,3,((0,7,6),(5,7,4))),
        (1,4,((1,6),)),
        (1,5,((1,0),)),
        (1,6,((3,6,5),(4,6,4,3))),
    ),
    (
        (0,0,((6,5,0,3),(6,3,1,3,6))),
        (0,1,((7,3,1),(7,7))),
        (0,2,((5,7,2,0),(0,7))),
        (0,3,((2,2),(7,5))),
        (0,4,((2,1,1),(2,4,0))),
        (0,5,((6,3),(1,3),(0,0))),
        (0,6,((0,6),)),
        (0,7,((2,2),(1,7,2,1))),
        (1,1,((5,0),)),
        (1,4,((2,5,3,4),(1,4))),
        (1,5,((5,6,5,3),(2,2,4,3))),
        (1,7,((1,0,3),(5,6,5),(7,1,3))),
    ),
    (
        (0,0,((1,5,5),)),
        (0,3,((2,7,0),)),
        (0,6,((0,1,1,0),)),
        (1,1,((6,1,3,5),)),
        (1,2,((3,5),)),
        (1,3,((1,6),(6,2,4,5))),
        (1,6,((3,7,5),(1,6,3))),
    ),
    (
        (0,0,((6,6,0,3),(4,3,4,6))),
        (0,1,((0,2),(3,1),(6,0,0))),
        (0,2,((3,0,2),(3,6),(6,5))),
        (0,3,((5,1,1),(5,3,0))),
        (0,4,((2,3,1),(1,1))),
        (0,5,((3,2),(1,4))),
        (0,6,((0,7,1),)),
        (0,7,((1,3,0),(2,0))),
        (1,2,((7,7,3),(1,2,4))),
        (1,3,((3,7),)),
        (1,4,((4,7),(6,0,3,4))),
        (1,5,((4,1,4),(2,4,5,3),(7,4,4,3))),
        (1,7,((4,1),(2,4,5))),
    ),
    (
        (0,3,((6,2),)),
        (0,6,((5,0),)),
        (1,1,((7,1),(1,3,3,5),(3,7))),
        (1,3,((4,7),(3,4,4,5))),
        (1,6,((2,1,4,3),(1,4,4),(4,7,3))),
    ),
    (
        (0,0,((7,0,5),(4,5,4,6))),
        (0,1,((7,5,2,1),(6,1))),
        (0,2,((4,0),(4,1,1))),
        (0,3,((5,6),(7,6))),
        (0,4,((2,6),(0,6,0))),
        (0,5,((6,5),(3,7,1))),
        (0,6,((5,6),)),
        (0,7,((2,6),)),
        (1,2,((5,4,4),(3,3,3))),
        (1,4,((0,4,6),(4,2,3,4))),
        (1,5,((3,0),(3,1))),
        (1,7,((2,6,3,4),(4,4,3),(5,4,4))),
    ),
    (
        (0,5,((7,4,1,0),)),
        (0,6,((0,2,1,0),)),
        (1,1,((2,3),)),
        (1,6,((2,3,4),)),
    ),
    (
        (0,0,((5,2,0,3),(7,2,4))),
        (0,1,((7,6,1),)),
        (0,2,((3,5),)),
        (0,3,((2,6),)),
        (0,4,((7,6),)),
        (0,5,((6,6),(1,6))),
        (0,6,((1,5),)),
        (0,7,((2,1),(1,4,0))),
        (1,1,((6,5,3,5),(5,1))),
        (1,2,((3,6,4,3),(5,7,5))),
        (1,3,((3,2,4,5),(1,1))),
        (1,4,((1,0),)),
        (1,5,((4,6,5),(7,7,4,3))),
        (1,6,((5,6,5),(5,0,4,3))),
        (1,7,((4,6,3),)),
    ),
    (
        (0,1,((3,2),(3,6))),
        (0,2,((4,4,1),)),
        (0,3,((5,5,0),)),
        (0,4,((2,5,0),)),
        (1,2,((4,2,5),)),
        (1,3,((5,6),)),
        (1,4,((6,4,3,4),(2,2))),
        (1,5,((2,5,5),)),
        (1,6,((5,1,5),)),
        (1,7,((2,5,5,4),)),
    ),
    (
        (0,6,((0,3,1),)),
        (0,7,((0,3),(2,3))),
        (1,1,((6,3,3,5),)),
        (1,2,((3,7),)),
        (1,3,((4,3,4,5),)),
        (1,4,((7,1),)),
        (1,5,((2,1,4),)),
        (1,6,((2,2,5,3),(7,1,4))),
    ),
    (
        (0,0,((2,7,0,3,5,6),(6,7,4,5,6),(2,0,1,3,5,6))),
        (0,1,((4,2),(6,5))),
        (0,2,((4,6),(4,7))),
        (0,3,((5,4,2,1),(1,7,0),(0,5))),
        (0,4,((3,3,1),(2,7,0))),
        (0,5,((0,4,0),(0,1))),
        (0,6,((1,7),)),
        (0,7,((0,0,0),)),
        (1,1,((5,6),)),
        (1,2,((6,2,4,5),(6,1,3))),
        (1,3,((2,4),(7,7))),
        (1,4,((1,5,3,4),)),
        (1,5,((6,0,5),)),
        (1,7,((6,2),(1,6),(6,0,5,4))),
    ),
    (
        (0,6,((5,5,0),)),
        (1,1,((6,6,3,5),(1,2,6))),
        (1,3,((4,5,4,5,6),)),
        (1,4,((4,1),(2,6,3))),
        (1,5,((3,3,4,3),)),
        (1,6,((2,6),(2,4,5))),
    ),
    (
        (0,0,((5,3,3,5,6),(7,3,4,5,6))),
        (0,1,((0,6),(6,6))),
        (0,2,((4,5,0),(5,2))),
        (0,3,((6,0),(5,7))),
        (0,4,((3,1),(1,2))),
        (0,5,((2,4),(0,7,1))),
        (0,6,((7,4),)),
        (0,7,((1,6,0),)),
        (1,1,((2,4),)),
        (1,2,((3,4,4,5,6),(1,3,3,6))),
        (1,4,((7,0,3,4),(7,4))),
        (1,5,((1,4,5),(4,2))),
        (1,7,((3,4,3,6),(2,1),(4,2,5))),
    ),
    (
        (0,6,((0,5,1,0),)),
        (1,1,((5,2,3,5),(5,4))),
        (1,3,((3,3,6),(7,2,4,5))),
        (1,4,((4,4),)),
        (1,6,((5,4,4),)),
    ),
    (
        (0,0,((5,5,3,5,6),(7,5,3,4,5))),
        (0,1,((4,1),(5,2))),
        (0,2,((7,1,0),(5,1))),
        (0,3,((6,4),)),
        (0,4,((3,5,1),(1,0))),
        (0,5,((7,5,1),(0,6),(0,2,1))),
        (0,7,((0,1,0),)),
        (1,2,((3,2,4,6),(6,5,3))),
        (1,3,((2,5),)),
        (1,5,((2,3),(6,1,3),(6,4,5))),
        (1,6,((7,4,3),)),
        (1,7,((3,2,3,4),(4,7),(6,4,5))),
    ),
    (
        (0,6,((0,4),(5,7))),
        (0,7,((3,3),)),
        (1,1,((4,6),)),
        (1,2,((5,6),)),
        (1,3,((3,6,6),)),
        (1,4,((7,7,4),)),
        (1,6,((5,7,4,3),(2,5,5))),
    ),
    (
        (0,0,((7,6,3,4,5,6),)),
        (0,1,((4,4),)),
        (0,2,((6,0),)),
        (0,3,((6,3),)),
        (0,4,((3,4,1),)),
        (0,5,((2,5),(0,3,1))),
        (0,7,((0,2),)),
        (1,1,((3,6),(2,7,3))),
        (1,2,((5,1,3),(4,3,4,6))),
        (1,3,((6,7,4,5),(6,0))),
        (1,4,((4,6),(2,7,3,4,6))),
        (1,5,((5,0),(1,3,4,3,6))),
        (1,6,((7,7),(4,2))),
        (1,7,((5,0,3),)),
    ),
    (
        (0,0,((1,7,3,4,5,6),)),
        (0,1,((2,7),)),
        (0,2,((5,4),)),
        (0,4,((1,3),)),
        (1,1,((2,5,6),(2,0,3,6))),
        (1,2,((6,3,3,5),(2,2))),
        (1,4,((6,7,3),(2,1))),
        (1,5,((1,5,5,3),)),
        (1,7,((1,5,5),(4,3,3,4,6))),
    ),
    (
        (0,3,((4,5),)),
        (0,6,((3,0),)),
        (1,1,((6,2),)),
        (1,3,((7,3,4,5),(6,1),(4,2,6))),
        (1,4,((3,4,6),)),
        (1,5,((7,1),)),
        (1,6,((6,0,5),(3,3,3))),
    ),
    (
        (0,3,((2,0),)),
        (0,4,((1,4),(3,7))),
        (0,5,((2,7),(0,5))),
        (0,7,((5,5,0),)),
        (1,1,((6,0,6),)),
        (1,2,((4,5,4,6),(6,6,3))),
        (1,4,((2,0,3,4,6),)),
        (1,5,((6,5,4,3),(2,6))),
        (1,7,((2,2,5),(4,5,3,4,6),(7,0,5,4))),
    ),
    (
        (0,3,((7,1),)),
        (0,4,((7,4),)),
        (0,7,((3,5),(5,4))),
        (1,1,((5,3,3,5,6),(3,4,6))),
        (1,3,((7,5),(1,3,6))),
        (1,4,((3,3),(3,2,6))),
        (1,6,((3,2,4,6),(6,2,4),(6,1,3))),
    ),
    (
        (0,4,((0,0),)),
        (0,7,((0,5,0),)),
        (1,1,((1,4),)),
        (1,2,((7,2,4),(5,2,3,5))),
        (1,3,((6,4,4),)),
        (1,5,((5,4),(6,3,4),(7,0,5))),
        (1,7,((7,4,5),(7,2,3,4))),
    ),
    (
        (0,7,((3,4),)),
        (1,2,((2,4),)),
        (1,3,((7,6,4,5),(6,5))),
        (1,4,((1,3,4,6),)),
        (1,6,((3,4,4,6),)),
        (1,7,((7,7),)),
    ),
    (
        (0,4,((0,7),(1,6))),
        (1,1,((3,2,6),(5,5,3))),
        (1,2,((6,7,4),)),
        (1,3,((1,5),)),
        (1,4,((5,3,4),(5,0))),
        (1,5,((5,7,5),(6,6,4,3),(6,7,6))),
        (1,6,((1,3,6),(4,3,4,6))),
        (1,7,((5,7,3),(6,7,4))),
    ),
    (
        (1,1,((6,4),(7,5,3))),
        (1,2,((2,5),)),
        (1,4,((7,3,3),(4,3,6),(6,5))),
    ),
    (
        (0,4,((7,5),)),
        (1,1,((4,3,6),)),
        (1,2,((2,7,3,6),(2,0,5,6),(7,3,4))),
        (1,3,((1,7,4,5,6),(5,1),(2,2))),
        (1,5,((5,2,4),)),
        (1,6,((6,3,3,6),(1,5,5),(4,5,6))),
        (1,7,((2,7,6),(2,0,5,6))),
    ),
    (
        (0,4,((0,1),)),
        (1,1,((1,5),)),
        (1,2,((6,0,6),)),
        (1,5,((3,2,6),)),
        (1,7,((3,3,6),(7,3,6))),
    ),
    (
        (1,1,((7,6,5,6),(4,5,5,6))),
        (1,3,((6,3,6),(7,0,6))),
        (1,4,((6,3),(4,5,6),(5,5,3,4))),
        (1,5,((2,7,3,6),(2,0,6),(6,2,4,6))),
        (1,6,((7,0,5),(6,5,3))),
    ),
    (
        (0,4,((0,2),(5,5))),
        (1,1,((7,0),)),
        (1,2,((6,4,5,6),(5,3,6))),
        (1,4,((7,5,3,4),)),
        (1,5,((5,3,3,6),)),
        (1,6,((5,2),)),
        (1,7,((6,1,3),(7,6,4))),
    ),
    (
        (1,1,((1,7,5,6),(7,2))),
        (1,3,((6,6,6),)),
        (1,4,((7,2,6),(6,6,6))),
        (1,7,((1,3,6),)),
    ),
    (
        (0,4,((0,3),(0,5))),
        (1,1,((5,7,6),)),
        (1,2,((7,6),)),
        (1,3,((7,4,6),)),
        (1,5,((7,3,3),(3,4,6))),
        (1,6,((6,6,3),(7,2,4))),
        (1,7,((6,3,6),)),
    ),
    (
        (1,2,((1,5),(5,5,3,5,6))),
        (1,3,((5,2,5),)),
        (1,4,((7,6,6),)),
        (1,6,((2,0,6),)),
        (1,7,((1,7,4,6),(5,3,5))),
    ),
    (
        (1,1,((6,7,6),)),
        (1,2,((7,5,5,6),(1,7,6))),
        (1,3,((2,0,6),)),
        (1,4,((5,7,6),(5,2,6))),
        (1,5,((4,3,6),)),
        (1,6,((6,7),)),
    ),
    (
        (1,2,((7,0,6),)),
        (1,4,((1,7,6),)),
        (1,7,((6,5),)),
    ),
    (
        (1,1,((7,3,6),)),
        (1,3,((2,7,6),)),
        (1,4,((6,1),(6,2,6))),
        (1,5,((7,6),(4,5,6),(5,5,6),(7,5,6))),
        (1,6,((6,4,6),)),
        (1,7,((5,5,6),)),
    ),
    (
        (1,5,((7,2,6),)),
        (1,6,((7,6),(2,7,6),(5,3,6))),
        (1,7,((7,5,6),)),
    ),
    (
        (1,7,((6,6,6),)),
    ),
    (
        (1,3,((5,3,6),)),
        (1,5,((1,7,6),)),
        (1,6,((1,7,6),(7,5,6))),
        (1,7,((5,2,6),)),
    ),
    (),
    (
        (1,3,((5,5,6),)),
        (1,6,((7,3,6),)),
    ),
    (
        (1,6,((5,5,6),)),
    ),
)
XP, XM, ZH, YP, YM, ZL, CORE = range(7)


def place():
    row, col = lax.axis_index("row"), lax.axis_index("col")
    return col // 2, lax.rem(col, 2), lax.rem(row // 2, 4), row // 8, lax.rem(row, 2)


def device(x, zh, y, zl, core):
    return (zl * 8 + y * 2 + core, x * 2 + zh)


def neighbours(x, zh, y, zl, core):
    def turn(a, by):
        return lax.rem(a + by, 4)

    return {
        XP: device(turn(x, 1), zh, y, zl, core),
        XM: device(turn(x, 3), zh, y, zl, core),
        ZH: device(x, 1 - zh, y, zl, core),
        YP: device(x, zh, turn(y, 1), zl, core),
        YM: device(x, zh, turn(y, 3), zl, core),
        ZL: device(x, zh, y, 1 - zl, core),
        CORE: device(x, zh, y, zl, 1 - core),
    }


def flip(a, b):
    return a + b - 2 * a * b


class Place:
    def __init__(self):
        self.coordinates = x, zh, y, zl, core = place()
        self.core = core
        self.row_root = (2 * zl + y // 2, lax.rem(y, 2))
        self.col_root = (2 * lax.rem(x, 2) + zh, x // 2)
        self.row_place = lax.rem(x - self.row_root[0] + 4, 4) + 4 * flip(zh, self.row_root[1])
        self.col_place = lax.rem(y - self.col_root[0] + 4, 4) + 4 * flip(zl, self.col_root[1])

    def row_shard(self, source):
        return lax.rem(self.row_root[0] + source % 4, 4) * 2 + flip(self.row_root[1], source // 4)

    def col_shard(self, source):
        return lax.rem(self.coordinates[0] + source % 4, 4) * 2 + flip(self.coordinates[1], source // 4)


def dot(lhs, rhs):
    return lax.dot_general(lhs, rhs, (((1,), (1,)), ((), ())), preferred_element_type=jnp.float32)


def clear_diagonal(block):
    same = lax.broadcasted_iota(jnp.int32, block.shape, 0) == lax.broadcasted_iota(jnp.int32, block.shape, 1)
    return jnp.where(same, 0.0, block.astype(jnp.float32)).astype(block.dtype)


def gather_kernel(
    pattern_hbm, weights_hbm, left, right, pattern_ref, weights_ref, in_sems, send_sems, row_sems, col_sems, core_sem
):
    loads = [
        pltpu.make_async_copy(weights_hbm, weights_ref, in_sems.at[0]),
        pltpu.make_async_copy(pattern_hbm, pattern_ref, in_sems.at[1]),
    ]
    for load in loads:
        load.start()
    reads, bins = weights_ref.shape
    section_count = pattern_ref.shape[1]
    bin_tile = bins // section_count
    piece = reads // CHUNKS
    x, zh, y, zl, core = place()
    near = neighbours(x, zh, y, zl, core)
    barrier = pltpu.get_barrier_semaphore()
    for target in near.values():
        pl.semaphore_signal(barrier, inc=1, device_id=target, device_id_type=MESH)
    own = pl.multiple_of((x * 2 + zh) * reads, reads)
    for load in loads:
        load.wait()
    for section in range(section_count):
        part = pl.ds(section * bin_tile, bin_tile)
        keep = pattern_ref[0, section].astype(jnp.float32)
        left[pl.ds(own, reads), part] = (weights_ref[:, part].astype(jnp.float32) * keep).astype(left.dtype)
    pl.semaphore_wait(barrier, len(near))

    here = Place()
    row_place, col_place = here.row_place, here.col_place
    row_source = [here.row_shard(s) for s in range(8)]
    col_source = [here.col_shard(s) for s in range(8)]
    row_tile = [pl.multiple_of(a * reads, reads) for a in row_source]
    col_tile = [pl.multiple_of((core * 8 + a) * reads, reads) for a in col_source]

    def in_left(s, c):
        return left.at[pl.ds(row_tile[s] + c * piece, piece)]

    def in_right(s, c):
        return right.at[pl.ds(col_tile[s] + c * piece, piece)]

    def copy(src, dst, way, recv_sem):
        return pltpu.make_async_remote_copy(
            src_ref=src, dst_ref=dst, send_sem=send_sems.at[way], recv_sem=recv_sem, device_id=near[way], device_id_type=MESH
        )

    def handle(kind, role, s, c, ways):
        row_sem = row_sems.at[row_source[s], c]
        col_sem = col_sems.at[col_source[s], c]
        if kind == 0:
            src = in_left(s, c)
            if s != role:
                copy(src, src, XP, row_sem).wait_recv()
        else:
            src = in_right(s, c)
            copy(src, src, YP, col_sem).wait_recv()
        for way in ways:
            if way <= ZH:
                copy(src, src, way, row_sem).start()
            elif way <= ZL:
                copy(src, in_right(s, c), way, col_sem).start()
            else:
                part = c * UNITS // CHUNKS
                start = part * (reads // UNITS)
                held = (left if kind == 0 else right).at[pl.ds((row_tile if kind == 0 else col_tile)[s] + start, reads // UNITS)]
                target = right.at[pl.ds(col_tile[s] + start, reads // UNITS)]
                copy(held, target, CORE, core_sem).start()
                if kind == 0:
                    target[...] = held[...]

    sent = {}

    def run_slot(slot):
        for kind, role, entries in SLOTS[slot]:
            for entry in entries:
                for way in entry[2:]:
                    at = (0 if way <= ZH else 1, role, way)
                    sent[at] = sent.get(at, 0) + 1

            @pl.when((row_place if kind == 0 else col_place) == role)
            def _(kind=kind, role=role, entries=entries):
                for entry in entries:
                    handle(kind, role, entry[0], entry[1], entry[2:])

    def dispatch(slot, low, high):
        if high - low == 1:
            run_slot(low)
            return
        middle = (low + high) // 2

        @pl.when(slot < middle)
        def _():
            dispatch(slot, low, middle)

        @pl.when(slot >= middle)
        def _():
            dispatch(slot, middle, high)

    @pl.loop(0, len(SLOTS))
    def _(slot):
        dispatch(slot, 0, len(SLOTS))

    for (kind, role, way), count in sorted(sent.items()):

        @pl.when((row_place if kind == 0 else col_place) == role)
        def _(way=way, count=count):
            block = right.at[pl.ds(0, 8 * reads if way == CORE else count * piece)]
            copy(block, block, way, core_sem).wait_send()
            if way == CORE:
                copy(block, block, way, core_sem).wait_recv()


def gather(tile_pattern, weights):
    reads, bins = weights.shape
    return pl.pallas_call(
        gather_kernel,
        out_shape=(pltpu.VMEM((8 * reads, bins), weights.dtype), pltpu.VMEM((16 * reads, bins), weights.dtype)),
        in_specs=[pl.BlockSpec(memory_space=pltpu.HBM), pl.BlockSpec(memory_space=pltpu.HBM)],
        out_specs=(pl.BlockSpec(memory_space=pltpu.VMEM),) * 2,
        scratch_shapes=[
            pltpu.SMEM(tile_pattern.shape, tile_pattern.dtype),
            pltpu.VMEM(weights.shape, weights.dtype),
            pltpu.SemaphoreType.DMA((2,)),
            pltpu.SemaphoreType.DMA((7,)),
            pltpu.SemaphoreType.DMA((8, CHUNKS)),
            pltpu.SemaphoreType.DMA((8, CHUNKS)),
            pltpu.SemaphoreType.DMA,
        ],
        compiler_params=pltpu.CompilerParams(collective_id=0, has_side_effects=True, vmem_limit_bytes=8 << 20),
        name="gather",
    )(*[pltpu.with_memory_space_constraint(a, pltpu.HBM) for a in (tile_pattern, weights)])


def product_kernel(scale, left, right, out, full, stage, sems):
    row, col = lax.axis_index("row"), lax.axis_index("col")
    slots, _, tile = stage.shape
    section_count = full.shape[1]
    bin_tile = left.shape[1] // section_count
    rows, cols = left.shape[0] // tile, right.shape[0] // tile

    def tile_at(index):
        return pl.ds(pl.multiple_of(index * tile, tile), tile)

    def write(j, slot):
        return pltpu.make_async_copy(stage.at[slot], out.at[:, tile_at(j)], sems.at[slot])

    for j in range(cols):
        for s in range(section_count):
            part = jnp.abs(right[pl.ds(j * tile, tile), pl.ds(s * bin_tile, bin_tile)]).reshape(-1, 16, bin_tile)
            top = jnp.max(jnp.max(part, axis=0).astype(jnp.float32))
            full[j, s] = (top > 0.0).astype(jnp.int32)

    @pl.loop(0, cols)
    def _(j):
        slot = lax.rem(j, slots)

        @pl.when(j >= slots)
        def _():
            write(j - slots, slot).wait()

        case = full[j, 0] + 2 * full[j, 1]

        def put(part):
            stage[slot] = (dot(left[:, part], right[tile_at(j), part]) * scale).astype(stage.dtype)

        @pl.when(case == 0)
        def _():
            stage[slot] = jnp.zeros(stage.shape[1:], stage.dtype)

        @pl.when(case == 1)
        def _():
            put(pl.ds(0, bin_tile))

        @pl.when(case == 2)
        def _():
            put(pl.ds(bin_tile, bin_tile))

        @pl.when(case == 3)
        def _():
            put(pl.ds(0, 2 * bin_tile))

        i = col * cols + j - row * rows

        @pl.when(jnp.logical_and(i >= 0, i < rows))
        def _():
            stage[slot, tile_at(i), :] = clear_diagonal(stage[slot, tile_at(i), :])

        write(j, slot).start()

    for j in range(cols - slots, cols):
        write(j, j % slots).wait()


def product(left, right, section_count):
    rows, cols = left.shape[0], right.shape[0]
    tile = rows // 8
    slots = 8

    def kernel(*refs):
        product_kernel(1.0 / math.sqrt(left.shape[1]), *refs)

    return pl.pallas_call(
        kernel,
        out_shape=jax.ShapeDtypeStruct((rows, cols), left.dtype),
        in_specs=[pl.BlockSpec(memory_space=pltpu.VMEM)] * 2,
        out_specs=pl.BlockSpec(memory_space=pl.ANY),
        scratch_shapes=[
            pltpu.SMEM((cols // tile, section_count), jnp.int32),
            pltpu.VMEM((slots, rows, tile), left.dtype),
            pltpu.SemaphoreType.DMA((slots,)),
        ],
        compiler_params=pltpu.CompilerParams(vmem_limit_bytes=24 << 20),
        name="product",
    )(left, right)


def shards(weights, tile_pattern):
    return product(*gather(tile_pattern, weights), tile_pattern.shape[1])


def solution(mesh):
    return jax.shard_map(
        shards,
        mesh=mesh,
        in_specs=(P(("row", "col"), None), P(("row", "col"), None)),
        out_specs=P("row", "col"),
        check_vma=False,
    )
```

```python
import math

import jax
import jax.numpy as jnp
from jax import lax
from jax.experimental import pallas as pl
from jax.experimental.pallas import tpu as pltpu
from jax.sharding import PartitionSpec as P

MESH = pl.DeviceIdType.MESH
CHUNKS = 8
UNITS = 2
SLOTS = (
    (
        (0,0,((0,0,1,5),(0,1,0,1,4),(0,2,1,4),(0,3,0,3,6),(0,4,0,1,4),(0,5,0,3),(0,6,1,5),(0,7,0,1,5,6))),
        (0,1,((1,0,0,1),(1,1,0,1,2),(1,2,0,1,2),(1,3,0),(1,4,0,1),(1,5,0,2),(1,6,0,1),(1,7,0,2))),
        (0,2,((2,0,1,2),(2,1,0,2),(2,2,1),(2,3,0,1,2),(2,4,0,2),(2,5,0,1,2),(2,6,1),(2,7,2))),
        (0,3,((3,0,0,2),(3,1,0,1,2),(3,2,2),(3,3,1),(3,4,1),(3,5,0),(3,6,0,2),(3,7,0,1,2))),
        (0,4,((4,0,0,2),(4,1,0,2),(4,2,0,1),(4,3,0,1),(4,4,1,2),(4,5,0,1),(4,6,0,1,2),(4,7,0,1,2))),
        (0,5,((5,0,1,2),(5,1,1),(5,2,0,1),(5,3,0,2),(5,4,0,1),(5,5,2),(5,6,1,2),(5,7,1,2))),
        (0,6,((6,0,0),(6,1,0,2),(6,2,1,2),(6,3,0,2),(6,4,1,2),(6,5,0),(6,6,0,2),(6,7,1,2))),
        (0,7,((7,0,1),(7,1,0,1),(7,2,0,1,2),(7,3,0,1),(7,4,2),(7,5,1),(7,6,1),(7,7,0,1,2))),
    ),
    (),
    (),
    (),
    (),
    (),
    (),
    (),
    (),
    (),
    (),
    (
        (1,4,((0,0,3),)),
        (0,0,((3,0,0,4),(1,0,1,3))),
        (0,1,((2,0),(0,1))),
        (0,2,((1,0,2),(3,1,2))),
        (0,3,((0,0,1),(2,1,0))),
        (0,4,((5,0,1),(7,1,0,2))),
        (0,5,((4,0,0,2),)),
        (0,6,((7,0,1,2),)),
        (0,7,((6,0,0),)),
    ),
    (
        (1,3,((0,1,4),)),
        (0,5,((6,2,1),)),
        (0,6,((5,2),)),
        (0,7,((4,2,1,2),)),
    ),
    (
        (1,1,((0,3,3),)),
        (0,0,((4,0,1,3,5),)),
        (0,1,((5,0,0,1),)),
        (0,6,((2,0,1),)),
        (0,7,((3,0,0),)),
    ),
    (
        (0,2,((6,1,0),)),
        (0,3,((7,2,1),)),
        (0,5,((1,1,0),)),
    ),
    (
        (1,4,((0,6,3,4),)),
        (0,0,((3,1,4),(1,1,5))),
        (0,1,((2,2,1,2),)),
        (0,2,((1,1,0),)),
        (0,3,((0,1,1),)),
        (0,4,((5,1,1,2),)),
        (0,5,((4,1,0),)),
        (0,6,((7,1),)),
        (0,7,((6,1,0),)),
    ),
    (
        (1,3,((0,2,4,5),)),
        (0,1,((0,3,0),)),
        (0,2,((3,3,1,2),)),
        (0,3,((2,3,0),)),
        (0,4,((7,2,0),)),
        (0,5,((6,4,1,2),)),
        (0,6,((5,3,0),)),
        (0,7,((4,3,2),)),
    ),
    (),
    (
        (1,1,((0,5,3,5),)),
        (0,0,((4,1,1,3),)),
        (0,1,((5,3,0),)),
        (0,2,((6,2,1),)),
        (0,5,((1,2,0),)),
        (0,6,((2,1,1),)),
        (0,7,((3,1),)),
    ),
    (
        (0,3,((7,4,0,1),)),
    ),
    (
        (1,4,((0,7,3,4),)),
        (0,0,((3,5,0,5),(1,2,1,5))),
        (0,1,((2,3),(0,4))),
        (0,2,((1,2),(3,4,1,2))),
        (0,3,((0,2,1),(2,4,0))),
        (0,4,((5,2,1),(7,3,0))),
        (0,5,((4,2),)),
        (0,6,((7,2),)),
        (0,7,((6,3,0),)),
    ),
    (
        (1,3,((0,4,4),)),
        (0,5,((6,7,1),)),
        (0,6,((5,4),)),
        (0,7,((4,4,1),)),
    ),
    (
        (0,0,((4,4,1,3),)),
        (0,1,((5,5,0),)),
        (0,6,((2,3,1),)),
        (0,7,((3,2,0,1),)),
    ),
    (
        (1,1,((1,0,3),)),
        (1,2,((0,1,4,5),)),
        (1,5,((0,0,5,3),)),
        (0,2,((6,3,1),)),
        (0,3,((7,7,0,1),)),
        (0,5,((1,5,1),)),
    ),
    (
        (1,2,((0,3,3,5),)),
        (0,0,((3,6,5),(1,4,1,4))),
        (0,1,((2,5),)),
        (0,2,((1,3,0,2),)),
        (0,3,((0,4,1,2),)),
        (0,4,((5,4,2),)),
        (0,5,((4,3,0,2),)),
        (0,6,((7,3,2),)),
        (0,7,((6,5,0,2),)),
    ),
    (
        (1,3,((3,0,4,5),)),
        (1,4,((4,0,3,4),)),
        (0,1,((0,5,0),)),
        (0,2,((3,7,1),)),
        (0,3,((2,5,0),)),
        (0,4,((7,7,0),)),
        (0,5,((7,0,1),)),
        (0,6,((4,0,0),)),
        (0,7,((4,5),)),
    ),
    (),
    (
        (1,1,((4,0,3),)),
        (1,5,((0,6),)),
        (1,7,((0,6,5,4),)),
        (0,0,((4,6,0,4),)),
        (0,1,((5,6,0,1),)),
        (0,2,((6,4),)),
        (0,5,((1,7,1),)),
        (0,6,((2,4,0),)),
        (0,7,((3,6,0,1),)),
    ),
    (
        (1,2,((0,2,4),)),
        (0,3,((4,2,0,1),)),
    ),
    (
        (1,2,((0,5,3),)),
        (1,4,((1,1,3,4),)),
        (0,0,((3,7,5),(1,6,3))),
        (0,1,((2,6,1,2),(0,7))),
        (0,2,((1,4,2),(0,0,1,2))),
        (0,3,((0,6,1,2),(6,1,0))),
        (0,4,((5,6,1),(6,0,0,2))),
        (0,5,((4,5,0,2),)),
        (0,6,((7,5,2),)),
        (0,7,((6,6,0),)),
    ),
    (
        (1,3,((3,1,4,5),)),
        (0,5,((2,0,1),)),
        (0,6,((1,1,0),)),
        (0,7,((4,6,1,2),)),
    ),
    (
        (0,0,((4,7,0,1,3),)),
        (0,1,((5,7,0,1),)),
        (0,6,((2,5,0),)),
        (0,7,((3,7,1),)),
    ),
    (
        (1,1,((4,1,3),)),
        (1,2,((0,4,4,5),)),
        (1,5,((0,7,5,3),)),
        (1,7,((0,7),)),
        (0,2,((6,6,0),)),
        (0,3,((4,3,1),)),
        (0,5,((2,2,0,1),)),
    ),
    (
        (0,0,((2,1,0,4),(5,0,1,4))),
        (0,1,((3,3,1,2),)),
        (0,2,((1,5,0),)),
        (0,3,((0,7,1,2),)),
        (0,4,((5,7,1),)),
        (0,5,((4,6),)),
        (0,6,((7,6,1,2),)),
        (0,7,((5,3,0),)),
    ),
    (
        (1,2,((1,0,3,5),)),
        (1,4,((3,5,3,4),)),
        (1,6,((0,0,3),)),
        (0,1,((3,0,0),)),
        (0,2,((7,2,1),)),
        (0,3,((1,1),)),
        (0,4,((3,0,0),)),
        (0,5,((2,1,1),)),
        (0,6,((4,1,0),)),
        (0,7,((4,7),)),
    ),
    (
        (1,1,((0,1),)),
        (1,6,((0,1,4,3),)),
    ),
    (
        (1,1,((4,4,3,5),)),
        (1,3,((1,4,4,5),)),
        (0,0,((7,1,4),)),
        (0,1,((4,0,0),)),
        (0,2,((6,7,0,1),)),
        (0,6,((2,7,0),)),
    ),
    (
        (1,2,((3,0,4),)),
        (1,3,((0,3),)),
        (1,5,((4,0),)),
        (1,7,((4,0,4),)),
    ),
    (
        (1,2,((4,0,3),)),
        (1,4,((1,2,3,4),)),
        (0,0,((2,3,4,5),(2,2,1,3))),
        (0,1,((6,2,1),(3,5,0,2))),
        (0,2,((1,6,0,2),(0,1,2))),
        (0,3,((1,0),(1,3,0))),
        (0,4,((6,2,1),(6,1,0))),
        (0,5,((4,7,0),)),
        (0,6,((7,7),)),
        (0,7,((4,0),)),
    ),
    (
        (1,6,((0,6,5),)),
        (0,5,((2,3,1),)),
        (0,6,((1,2,0),)),
        (0,7,((5,0),)),
    ),
    (
        (1,5,((0,5,4,3),)),
        (1,7,((0,2,3,4),)),
        (0,0,((5,1,0,1,5),)),
        (0,1,((6,4,1),)),
        (0,3,((6,5,1,0),)),
        (0,6,((1,0,1,0),)),
        (0,7,((0,4,0),)),
    ),
    (
        (1,1,((0,0,3),(0,2,6),(1,6,3,5))),
        (1,2,((3,1,4),)),
        (1,3,((4,6,4),(0,5))),
        (1,5,((1,1,5),)),
        (1,7,((1,1,4),)),
        (0,2,((7,0,0,1),)),
    ),
    (
        (1,6,((0,3,4,3),)),
        (0,0,((7,4,0,3),(5,6,1,5))),
        (0,1,((3,4,1),)),
        (0,2,((1,7),)),
        (0,3,((4,0),)),
        (0,4,((6,4,1),)),
        (0,5,((7,1,2),)),
        (0,6,((4,2),)),
        (0,7,((2,4,0),)),
    ),
    (
        (1,4,((3,6,3,4),)),
        (0,1,((4,6,0),)),
        (0,2,((7,4),)),
        (0,3,((6,6,0),)),
        (0,4,((6,3,0),)),
        (0,6,((4,3),)),
        (0,7,((5,1,1),)),
    ),
    (
        (0,5,((2,6,0,1),(7,6,1))),
    ),
    (
        (1,1,((0,4),(4,7,3,5))),
        (1,2,((4,1,3,5),)),
        (1,3,((2,1,4),(0,6))),
        (1,6,((0,7,5),)),
        (1,7,((0,0),)),
        (0,6,((3,1,1),)),
    ),
    (
        (1,3,((1,0),)),
        (1,5,((3,5,5),(0,1))),
        (1,7,((3,5,5,4),)),
    ),
    (
        (1,2,((1,4),)),
        (1,4,((3,7,3,4),)),
        (0,0,((2,4,0,5),(2,6,1,3,4))),
        (0,1,((6,3,1),(4,7))),
        (0,2,((5,0,2),(7,3,0,1),(0,2,1,2))),
        (0,3,((4,1,1),(4,6),(1,5,2))),
        (0,4,((6,7,1),(3,2,2,0))),
        (0,5,((7,2),)),
        (0,6,((4,4,1),)),
        (0,7,((1,1,0),(0,6,0,1))),
    ),
    (
        (1,6,((4,0),)),
        (0,1,((4,3,1),)),
        (0,5,((3,3,1),)),
        (0,6,((4,5),)),
        (0,7,((5,2,2),)),
    ),
    (
        (1,2,((4,4,3),)),
        (1,7,((3,0,3,4),)),
        (0,0,((5,4,0,1,4,5),)),
        (0,6,((3,3),)),
    ),
    (
        (1,1,((2,2,5),(3,0))),
        (1,3,((5,0,4),(4,0))),
        (1,5,((1,2,3),)),
        (1,7,((0,1,3),(1,2,5))),
    ),
    (
        (0,0,((7,7,0,3),(5,7,4))),
        (0,1,((3,7),)),
        (0,2,((0,3,0,2),)),
        (0,3,((1,2),)),
        (0,4,((1,5,2),)),
        (0,5,((7,3),(1,0))),
        (0,6,((3,2,2),)),
        (0,7,((2,5,0),(0,7,1))),
    ),
    (
        (1,2,((0,6,4),(4,6,5))),
        (1,4,((2,3,4),)),
        (0,1,((2,1),)),
        (0,2,((7,7),)),
        (0,3,((6,7),)),
        (0,4,((6,5,0),)),
        (0,6,((2,2,0),)),
        (0,7,((5,6,1),)),
    ),
    (
        (1,4,((0,2,3),(0,5))),
        (1,6,((0,5,3),(0,2,6))),
    ),
    (
        (1,1,((3,1),(7,4,3,5))),
        (1,2,((0,0,3,6),)),
        (1,3,((7,1,4,5),)),
        (1,5,((4,4,3),)),
        (0,2,((7,5,0,1),)),
        (0,6,((3,4,1),)),
    ),
    (
        (1,5,((3,6,3),(0,3,4))),
        (1,6,((0,4,4,3,6),)),
        (1,7,((3,6),(0,3,6))),
        (0,1,((4,5,1,0),)),
    ),
    (
        (1,1,((0,7),)),
        (1,3,((4,1),)),
        (1,4,((5,1,3,4),)),
        (0,0,((2,5,5),(3,3,3),(6,0,1,0,5))),
        (0,1,((0,0,2),(5,1))),
        (0,2,((5,3,0),(0,4))),
        (0,3,((4,4,1),(1,6))),
        (0,4,((7,0),(3,6))),
        (0,5,((7,7),(3,1,2,1))),
        (0,6,((3,6,2,1),)),
        (0,7,((4,1),)),
    ),
    (
        (1,2,((2,1,4,5),(0,7,3,6))),
        (0,6,((4,7),)),
        (0,7,((5,7),)),
    ),
    (
        (1,2,((1,6,3),)),
        (1,6,((1,1,5),)),
        (1,7,((3,1,3,4),)),
        (0,5,((3,5,1,0),)),
        (0,6,((1,3,1,0),)),
    ),
    (
        (1,1,((2,6,3),)),
        (1,3,((2,3,4),)),
        (1,5,((1,6,4,3),)),
        (0,2,((7,6,0,1),)),
    ),
    (
        (1,3,((3,5,4),)),
        (1,5,((3,7,5),)),
        (1,6,((1,0,4,3),)),
        (0,0,((4,2,3,5),(6,2,4))),
        (0,1,((7,2,1),)),
        (0,2,((5,5,2,0),)),
        (0,3,((1,4),)),
        (0,4,((1,7,1),)),
        (0,5,((6,0),(4,4))),
        (0,6,((4,6),)),
        (0,7,((2,7,2,0),)),
    ),
    (
        (1,1,((1,1),)),
        (1,3,((4,4),)),
        (1,4,((5,6,3,4),)),
        (1,7,((3,7,5,4),)),
        (0,1,((7,4,2),)),
        (0,2,((4,2,1),)),
        (0,3,((7,0,0),)),
        (0,4,((6,6,0),)),
        (0,6,((2,6,0),)),
        (0,7,((6,2,2),)),
    ),
    (
        (1,2,((5,0,4,5),)),
        (1,4,((3,0),)),
        (1,6,((3,5),)),
    ),
    (
        (1,1,((7,7,3,5),)),
        (1,2,((4,7,3),)),
        (1,3,((2,6,5),)),
        (1,6,((1,2,5),)),
        (1,7,((1,4,3,4),)),
        (0,6,((1,4,1,0),)),
    ),
    (
        (1,1,((0,6,6),)),
        (1,7,((0,5),)),
    ),
    (
        (1,4,((2,4,3,4),)),
        (1,5,((4,7,4,3),(0,2,6))),
        (1,7,((2,3,4),)),
        (0,0,((6,1,0,3),(6,4,1,5))),
        (0,1,((6,7,1),(2,4))),
        (0,2,((0,5,0,2),(0,6,1))),
        (0,3,((4,7,1),(7,3))),
        (0,4,((2,0,2,1),(5,3))),
        (0,5,((3,0),(3,4,1))),
        (0,6,((3,7,1),)),
        (0,7,((1,2,0),)),
    ),
    (
        (1,2,((7,1,4,5),)),
        (1,4,((0,1),)),
        (1,6,((4,1,4,3),)),
        (0,1,((7,1,0),)),
        (0,3,((5,2,1,0),)),
        (0,7,((6,4),)),
    ),
    (
        (1,1,((3,5),)),
        (1,3,((0,0,6),)),
        (1,4,((0,3,6),)),
        (1,5,((0,4,4,6),)),
        (1,6,((3,0,4),(4,4,3))),
        (0,6,((0,0,0),)),
    ),
    (
        (1,1,((3,3,3,5),)),
        (1,2,((7,4),)),
        (1,3,((5,4,4),(1,2))),
        (0,7,((1,5,1),)),
    ),
    (
        (1,7,((0,4,6),)),
        (0,0,((1,3,3,6),(3,4,4,6))),
        (0,1,((7,0),)),
        (0,2,((5,6),)),
        (0,3,((5,0),)),
        (0,4,((2,2),)),
        (0,5,((6,1),(3,6,2))),
        (0,6,((5,1),)),
        (0,7,((1,0,0),)),
    ),
    (
        (1,1,((2,1),)),
        (1,4,((5,4,4),)),
        (1,5,((5,1,5),)),
        (1,7,((5,1,4),)),
        (0,1,((5,4),)),
        (0,2,((4,3),)),
        (0,3,((0,3,2),)),
        (0,4,((0,4,0),)),
        (0,7,((6,7),)),
    ),
    (
        (1,4,((3,1,3),)),
        (1,6,((3,1),)),
    ),
    (
        (1,1,((4,2,3),)),
        (1,2,((2,3,4),(1,1,3))),
        (1,3,((0,7,6),(5,7,4))),
        (1,4,((1,6),)),
        (1,6,((3,6,5),)),
        (0,0,((3,2,0,4,6),)),
        (0,2,((3,2),)),
        (0,6,((3,5),(1,6,1,0))),
    ),
    (
        (1,2,((2,6),)),
        (1,5,((1,0),)),
        (1,6,((4,6,4,3),)),
    ),
    (
        (1,1,((5,0),)),
        (1,4,((2,5,3,4),)),
        (1,5,((5,6,5,3),)),
        (1,7,((1,0,3),(5,6,5))),
        (0,0,((6,5,0,3),(6,3,1,3,6))),
        (0,1,((7,3,1),(7,7))),
        (0,2,((5,7,2,0),(0,7))),
        (0,3,((2,2),(7,5))),
        (0,4,((2,1,1),(2,4,0))),
        (0,5,((6,3),(1,3))),
        (0,6,((0,6),)),
        (0,7,((2,2),)),
    ),
    (
        (1,4,((1,4),)),
        (1,5,((2,2,4,3),)),
        (1,7,((7,1,3),)),
        (0,5,((0,0),)),
        (0,7,((1,7,2,1),)),
    ),
    (
        (1,2,((3,5),)),
        (1,3,((1,6),)),
        (1,6,((3,7,5),(1,6,3))),
        (0,0,((1,5,5),)),
        (0,3,((2,7,0),)),
        (0,6,((0,1,1,0),)),
    ),
    (
        (1,1,((6,1,3,5),)),
        (1,3,((6,2,4,5),)),
    ),
    (
        (1,2,((7,7,3),)),
        (1,3,((3,7),)),
        (1,4,((4,7),)),
        (1,5,((4,1,4),)),
        (1,7,((4,1),)),
        (0,0,((6,6,0,3),(4,3,4,6))),
        (0,1,((0,2),(3,1))),
        (0,2,((3,0,2),)),
        (0,3,((5,1,1),)),
        (0,4,((2,3,1),)),
        (0,5,((3,2),(1,4))),
        (0,6,((0,7,1),)),
        (0,7,((1,3,0),)),
    ),
    (
        (1,2,((1,2,4),)),
        (1,4,((6,0,3,4),)),
        (1,5,((2,4,5,3),(7,4,4,3))),
        (1,7,((2,4,5),)),
        (0,1,((6,0,0),)),
        (0,2,((3,6),(6,5))),
        (0,3,((5,3,0),)),
        (0,4,((1,1),)),
        (0,7,((2,0),)),
    ),
    (
        (1,1,((7,1),)),
        (1,6,((2,1,4,3),(1,4,4))),
        (0,3,((6,2),)),
    ),
    (
        (1,1,((1,3,3,5),(3,7))),
        (1,3,((4,7),(3,4,4,5))),
        (1,6,((4,7,3),)),
        (0,6,((5,0),)),
    ),
    (
        (1,4,((0,4,6),)),
        (1,5,((3,0),)),
        (1,7,((2,6,3,4),)),
    ),
    (
        (1,2,((5,4,4),(3,3,3))),
        (1,4,((4,2,3,4),)),
        (1,5,((3,1),)),
        (1,7,((4,4,3),(5,4,4))),
        (0,0,((7,0,5),(4,5,4,6))),
        (0,1,((7,5,2,1),(6,1))),
        (0,2,((4,0),(4,1,1))),
        (0,3,((5,6),(7,6))),
        (0,4,((2,6),(0,6,0))),
        (0,5,((6,5),(3,7,1))),
        (0,6,((5,6),)),
        (0,7,((2,6),)),
    ),
    (
        (0,5,((7,4,1,0),)),
    ),
    (
        (1,1,((2,3),)),
        (1,6,((2,3,4),)),
        (0,6,((0,2,1,0),)),
    ),
    (
        (1,1,((6,5,3,5),)),
        (1,3,((3,2,4,5),(1,1))),
        (1,4,((1,0),)),
        (1,6,((5,6,5),)),
        (0,7,((2,1),)),
    ),
    (
        (1,1,((5,1),)),
        (1,2,((3,6,4,3),(5,7,5))),
        (1,5,((4,6,5),(7,7,4,3))),
        (1,6,((5,0,4,3),)),
        (1,7,((4,6,3),)),
        (0,0,((5,2,0,3),(7,2,4))),
        (0,1,((7,6,1),)),
        (0,2,((3,5),)),
        (0,3,((2,6),)),
        (0,4,((7,6),)),
        (0,5,((6,6),(1,6))),
        (0,6,((1,5),)),
        (0,7,((1,4,0),)),
    ),
    (
        (1,2,((4,2,5),)),
        (1,3,((5,6),)),
        (1,4,((6,4,3,4),)),
        (1,5,((2,5,5),)),
        (1,7,((2,5,5,4),)),
        (0,1,((3,2),(3,6))),
        (0,2,((4,4,1),)),
        (0,3,((5,5,0),)),
        (0,4,((2,5,0),)),
    ),
    (
        (1,4,((2,2),)),
        (1,6,((5,1,5),)),
    ),
    (
        (1,1,((6,3,3,5),)),
        (1,3,((4,3,4,5),)),
        (1,4,((7,1),)),
        (0,6,((0,3,1),)),
        (0,7,((0,3),(2,3))),
    ),
    (
        (1,2,((3,7),)),
        (1,5,((2,1,4),)),
        (1,6,((2,2,5,3),(7,1,4))),
    ),
    (
        (1,2,((6,2,4,5),(6,1,3))),
        (1,3,((2,4),)),
        (1,4,((1,5,3,4),)),
        (1,5,((6,0,5),)),
        (1,7,((6,2),(1,6),(6,0,5,4))),
        (0,0,((2,7,0,3,5,6),(6,7,4,5,6),(2,0,1,3,5,6))),
        (0,1,((4,2),(6,5))),
        (0,2,((4,6),(4,7))),
        (0,3,((5,4,2,1),(1,7,0),(0,5))),
        (0,4,((3,3,1),(2,7,0))),
        (0,5,((0,4,0),(0,1))),
        (0,6,((1,7),)),
        (0,7,((0,0,0),)),
    ),
    (
        (1,1,((5,6),)),
        (1,3,((7,7),)),
    ),
    (
        (1,6,((2,6),)),
        (0,6,((5,5,0),)),
    ),
    (
        (1,1,((6,6,3,5),(1,2,6))),
        (1,3,((4,5,4,5,6),)),
        (1,4,((4,1),(2,6,3))),
        (1,5,((3,3,4,3),)),
        (1,6,((2,4,5),)),
    ),
    (
        (1,2,((3,4,4,5,6),)),
        (1,5,((1,4,5),)),
        (1,7,((3,4,3,6),(2,1))),
        (0,0,((5,3,3,5,6),(7,3,4,5,6))),
        (0,1,((0,6),)),
        (0,2,((4,5,0),)),
        (0,3,((6,0),)),
        (0,4,((3,1),)),
        (0,5,((2,4),(0,7,1))),
        (0,7,((1,6,0),)),
    ),
    (
        (1,1,((2,4),)),
        (1,2,((1,3,3,6),)),
        (1,4,((7,0,3,4),(7,4))),
        (1,5,((4,2),)),
        (1,7,((4,2,5),)),
        (0,1,((6,6),)),
        (0,2,((5,2),)),
        (0,3,((5,7),)),
        (0,4,((1,2),)),
        (0,6,((7,4),)),
    ),
    (
        (1,3,((3,3,6),)),
    ),
    (
        (1,1,((5,2,3,5),(5,4))),
        (1,3,((7,2,4,5),)),
        (1,4,((4,4),)),
        (1,6,((5,4,4),)),
        (0,6,((0,5,1,0),)),
    ),
    (
        (1,3,((2,5),)),
        (1,5,((2,3),)),
        (1,6,((7,4,3),)),
        (0,5,((7,5,1),)),
    ),
    (
        (1,2,((3,2,4,6),(6,5,3))),
        (1,5,((6,1,3),(6,4,5))),
        (1,7,((3,2,3,4),(4,7),(6,4,5))),
        (0,0,((5,5,3,5,6),(7,5,3,4,5))),
        (0,1,((4,1),(5,2))),
        (0,2,((7,1,0),(5,1))),
        (0,3,((6,4),)),
        (0,4,((3,5,1),(1,0))),
        (0,5,((0,6),(0,2,1))),
        (0,7,((0,1,0),)),
    ),
    (
        (1,1,((4,6),)),
        (1,6,((5,7,4,3),)),
    ),
    (
        (1,2,((5,6),)),
        (1,3,((3,6,6),)),
        (1,4,((7,7,4),)),
        (1,6,((2,5,5),)),
        (0,6,((0,4),(5,7))),
        (0,7,((3,3),)),
    ),
    (
        (1,1,((3,6),)),
        (1,3,((6,7,4,5),(6,0))),
        (1,4,((4,6),)),
        (1,6,((7,7),)),
    ),
    (
        (1,1,((2,7,3),)),
        (1,2,((5,1,3),(4,3,4,6))),
        (1,4,((2,7,3,4,6),)),
        (1,5,((5,0),(1,3,4,3,6))),
        (1,6,((4,2),)),
        (1,7,((5,0,3),)),
        (0,0,((7,6,3,4,5,6),)),
        (0,1,((4,4),)),
        (0,2,((6,0),)),
        (0,3,((6,3),)),
        (0,4,((3,4,1),)),
        (0,5,((2,5),(0,3,1))),
        (0,7,((0,2),)),
    ),
    (
        (1,1,((2,5,6),)),
        (1,2,((6,3,3,5),)),
        (1,5,((1,5,5,3),)),
        (1,7,((1,5,5),(4,3,3,4,6))),
        (0,0,((1,7,3,4,5,6),)),
        (0,1,((2,7),)),
        (0,2,((5,4),)),
        (0,4,((1,3),)),
    ),
    (
        (1,1,((2,0,3,6),)),
        (1,2,((2,2),)),
        (1,4,((6,7,3),(2,1))),
    ),
    (
        (1,3,((7,3,4,5),(6,1))),
        (1,4,((3,4,6),)),
        (1,6,((6,0,5),)),
        (0,3,((4,5),)),
        (0,6,((3,0),)),
    ),
    (
        (1,1,((6,2),)),
        (1,3,((4,2,6),)),
        (1,5,((7,1),)),
        (1,6,((3,3,3),)),
    ),
    (
        (1,2,((4,5,4,6),(6,6,3))),
        (1,5,((6,5,4,3),(2,6))),
        (1,7,((2,2,5),(4,5,3,4,6))),
        (0,3,((2,0),)),
        (0,4,((1,4),)),
        (0,5,((2,7),(0,5))),
        (0,7,((5,5,0),)),
    ),
    (
        (1,1,((6,0,6),)),
        (1,4,((2,0,3,4,6),)),
        (1,7,((7,0,5,4),)),
        (0,4,((3,7),)),
    ),
    (
        (1,4,((3,3),)),
        (1,6,((3,2,4,6),)),
        (0,7,((3,5),)),
    ),
    (
        (1,1,((5,3,3,5,6),(3,4,6))),
        (1,3,((7,5),(1,3,6))),
        (1,4,((3,2,6),)),
        (1,6,((6,2,4),(6,1,3))),
        (0,3,((7,1),)),
        (0,4,((7,4),)),
        (0,7,((5,4),)),
    ),
    (
        (1,2,((7,2,4),)),
        (1,3,((6,4,4),)),
        (1,5,((5,4),(6,3,4))),
        (1,7,((7,4,5),)),
        (0,7,((0,5,0),)),
    ),
    (
        (1,1,((1,4),)),
        (1,2,((5,2,3,5),)),
        (1,5,((7,0,5),)),
        (1,7,((7,2,3,4),)),
        (0,4,((0,0),)),
    ),
    (
        (1,2,((2,4),)),
        (1,7,((7,7),)),
    ),
    (
        (1,3,((7,6,4,5),(6,5))),
        (1,4,((1,3,4,6),)),
        (1,6,((3,4,4,6),)),
        (0,7,((3,4),)),
    ),
    (
        (1,1,((3,2,6),(5,5,3))),
        (1,3,((1,5),)),
        (1,4,((5,3,4),)),
        (1,6,((1,3,6),(4,3,4,6))),
    ),
    (
        (1,2,((6,7,4),)),
        (1,4,((5,0),)),
        (1,5,((5,7,5),(6,6,4,3),(6,7,6))),
        (1,7,((5,7,3),(6,7,4))),
        (0,4,((0,7),(1,6))),
    ),
    (
        (1,1,((6,4),)),
        (1,4,((7,3,3),)),
    ),
    (
        (1,1,((7,5,3),)),
        (1,2,((2,5),)),
        (1,4,((4,3,6),(6,5))),
    ),
    (
        (1,1,((4,3,6),)),
        (1,2,((2,7,3,6),(2,0,5,6))),
        (1,3,((1,7,4,5,6),(5,1))),
        (1,6,((6,3,3,6),(1,5,5))),
    ),
    (
        (1,2,((7,3,4),)),
        (1,3,((2,2),)),
        (1,5,((5,2,4),)),
        (1,6,((4,5,6),)),
        (1,7,((2,7,6),(2,0,5,6))),
        (0,4,((7,5),)),
    ),
    (
        (1,1,((1,5),)),
        (1,7,((3,3,6),(7,3,6))),
        (0,4,((0,1),)),
    ),
    (
        (1,2,((6,0,6),)),
        (1,5,((3,2,6),)),
    ),
    (
        (1,1,((7,6,5,6),)),
        (1,3,((6,3,6),)),
        (1,4,((6,3),)),
        (1,5,((2,7,3,6),(2,0,6))),
    ),
    (
        (1,1,((4,5,5,6),)),
        (1,3,((7,0,6),)),
        (1,4,((4,5,6),(5,5,3,4))),
        (1,5,((6,2,4,6),)),
        (1,6,((7,0,5),(6,5,3))),
    ),
    (
        (1,2,((6,4,5,6),)),
        (1,5,((5,3,3,6),)),
        (1,6,((5,2),)),
        (1,7,((6,1,3),)),
        (0,4,((0,2),(5,5))),
    ),
    (
        (1,1,((7,0),)),
        (1,2,((5,3,6),)),
        (1,4,((7,5,3,4),)),
        (1,7,((7,6,4),)),
    ),
    (
        (1,7,((1,3,6),)),
    ),
    (
        (1,1,((1,7,5,6),(7,2))),
        (1,3,((6,6,6),)),
        (1,4,((7,2,6),(6,6,6))),
    ),
    (
        (1,3,((7,4,6),)),
        (1,6,((6,6,3),(7,2,4))),
        (0,4,((0,3),)),
    ),
    (
        (1,1,((5,7,6),)),
        (1,2,((7,6),)),
        (1,5,((7,3,3),(3,4,6))),
        (1,7,((6,3,6),)),
        (0,4,((0,5),)),
    ),
    (
        (1,6,((2,0,6),)),
        (1,7,((1,7,4,6),(5,3,5))),
    ),
    (
        (1,2,((1,5),(5,5,3,5,6))),
        (1,3,((5,2,5),)),
        (1,4,((7,6,6),)),
    ),
    (
        (1,1,((6,7,6),)),
        (1,2,((7,5,5,6),)),
        (1,3,((2,0,6),)),
        (1,4,((5,7,6),(5,2,6))),
        (1,6,((6,7),)),
    ),
    (
        (1,2,((1,7,6),)),
        (1,5,((4,3,6),)),
    ),
    (),
    (
        (1,2,((7,0,6),)),
        (1,4,((1,7,6),)),
        (1,7,((6,5),)),
    ),
    (
        (1,1,((7,3,6),)),
        (1,3,((2,7,6),)),
        (1,4,((6,1),)),
        (1,5,((7,6),(4,5,6))),
    ),
    (
        (1,4,((6,2,6),)),
        (1,5,((5,5,6),(7,5,6))),
        (1,6,((6,4,6),)),
        (1,7,((5,5,6),)),
    ),
    (
        (1,6,((7,6),)),
        (1,7,((7,5,6),)),
    ),
    (
        (1,5,((7,2,6),)),
        (1,6,((2,7,6),(5,3,6))),
    ),
    (
        (1,7,((6,6,6),)),
    ),
    (),
    (
        (1,3,((5,3,6),)),
        (1,6,((1,7,6),)),
    ),
    (
        (1,5,((1,7,6),)),
        (1,6,((7,5,6),)),
        (1,7,((5,2,6),)),
    ),
    (),
    (),
    (
        (1,3,((5,5,6),)),
        (1,6,((7,3,6),)),
    ),
    (),
    (
        (1,6,((5,5,6),)),
    ),
)
XP, XM, ZH, YP, YM, ZL, CORE = range(7)


def place():
    row, col = lax.axis_index("row"), lax.axis_index("col")
    return col // 2, lax.rem(col, 2), lax.rem(row // 2, 4), row // 8, lax.rem(row, 2)


def device(x, zh, y, zl, core):
    return (zl * 8 + y * 2 + core, x * 2 + zh)


def neighbours(x, zh, y, zl, core):
    def turn(a, by):
        return lax.rem(a + by, 4)

    return {
        XP: device(turn(x, 1), zh, y, zl, core),
        XM: device(turn(x, 3), zh, y, zl, core),
        ZH: device(x, 1 - zh, y, zl, core),
        YP: device(x, zh, turn(y, 1), zl, core),
        YM: device(x, zh, turn(y, 3), zl, core),
        ZL: device(x, zh, y, 1 - zl, core),
        CORE: device(x, zh, y, zl, 1 - core),
    }


def flip(a, b):
    return a + b - 2 * a * b


class Place:
    def __init__(self):
        self.coordinates = x, zh, y, zl, core = place()
        self.core = core
        self.row_root = (2 * zl + y // 2, lax.rem(y, 2))
        self.col_root = (2 * lax.rem(x, 2) + zh, x // 2)
        self.row_place = lax.rem(x - self.row_root[0] + 4, 4) + 4 * flip(zh, self.row_root[1])
        self.col_place = lax.rem(y - self.col_root[0] + 4, 4) + 4 * flip(zl, self.col_root[1])

    def row_shard(self, source):
        return lax.rem(self.row_root[0] + source % 4, 4) * 2 + flip(self.row_root[1], source // 4)

    def col_shard(self, source):
        return lax.rem(self.coordinates[0] + source % 4, 4) * 2 + flip(self.coordinates[1], source // 4)


def dot(lhs, rhs):
    return lax.dot_general(lhs, rhs, (((1,), (1,)), ((), ())), preferred_element_type=jnp.float32)


def clear_diagonal(block):
    same = lax.broadcasted_iota(jnp.int32, block.shape, 0) == lax.broadcasted_iota(jnp.int32, block.shape, 1)
    return jnp.where(same, 0.0, block.astype(jnp.float32)).astype(block.dtype)


def gather_kernel(
    pattern_hbm, weights_hbm, left, right, pattern_ref, weights_ref, in_sems, send_sems, row_sems, col_sems, core_sem
):
    loads = [
        pltpu.make_async_copy(weights_hbm, weights_ref, in_sems.at[0]),
        pltpu.make_async_copy(pattern_hbm, pattern_ref, in_sems.at[1]),
    ]
    for load in loads:
        load.start()
    reads, bins = weights_ref.shape
    section_count = pattern_ref.shape[1]
    bin_tile = bins // section_count
    piece = reads // CHUNKS
    x, zh, y, zl, core = place()
    near = neighbours(x, zh, y, zl, core)
    barrier = pltpu.get_barrier_semaphore()
    for target in near.values():
        pl.semaphore_signal(barrier, inc=1, device_id=target, device_id_type=MESH)
    own = pl.multiple_of((x * 2 + zh) * reads, reads)
    for load in loads:
        load.wait()
    for section in range(section_count):
        part = pl.ds(section * bin_tile, bin_tile)
        keep = pattern_ref[0, section].astype(jnp.float32)
        left[pl.ds(own, reads), part] = (weights_ref[:, part].astype(jnp.float32) * keep).astype(left.dtype)
    pl.semaphore_wait(barrier, len(near))

    here = Place()
    row_place, col_place = here.row_place, here.col_place
    row_source = [here.row_shard(s) for s in range(8)]
    col_source = [here.col_shard(s) for s in range(8)]
    row_tile = [pl.multiple_of(a * reads, reads) for a in row_source]
    col_tile = [pl.multiple_of((core * 8 + a) * reads, reads) for a in col_source]

    def in_left(s, c):
        return left.at[pl.ds(row_tile[s] + c * piece, piece)]

    def in_right(s, c):
        return right.at[pl.ds(col_tile[s] + c * piece, piece)]

    def copy(src, dst, way, recv_sem):
        return pltpu.make_async_remote_copy(
            src_ref=src, dst_ref=dst, send_sem=send_sems.at[way], recv_sem=recv_sem, device_id=near[way], device_id_type=MESH
        )

    def handle(kind, role, s, c, ways):
        row_sem = row_sems.at[row_source[s], c]
        col_sem = col_sems.at[col_source[s], c]
        if kind == 0:
            src = in_left(s, c)
            if s != role:
                copy(src, src, XP, row_sem).wait_recv()
        else:
            src = in_right(s, c)
            copy(src, src, YP, col_sem).wait_recv()
        for way in ways:
            if way <= ZH:
                copy(src, src, way, row_sem).start()
            elif way <= ZL:
                copy(src, in_right(s, c), way, col_sem).start()
            else:
                part = c * UNITS // CHUNKS
                start = part * (reads // UNITS)
                held = (left if kind == 0 else right).at[pl.ds((row_tile if kind == 0 else col_tile)[s] + start, reads // UNITS)]
                target = right.at[pl.ds(col_tile[s] + start, reads // UNITS)]
                copy(held, target, CORE, core_sem).start()
                if kind == 0:
                    target[...] = held[...]

    sent = {}

    def run_slot(slot):
        for kind, role, entries in SLOTS[slot]:
            for entry in entries:
                for way in entry[2:]:
                    at = (0 if way <= ZH else 1, role, way)
                    sent[at] = sent.get(at, 0) + 1

            @pl.when((row_place if kind == 0 else col_place) == role)
            def _(kind=kind, role=role, entries=entries):
                for entry in entries:
                    handle(kind, role, entry[0], entry[1], entry[2:])

    def dispatch(slot, low, high):
        if high - low == 1:
            run_slot(low)
            return
        middle = (low + high) // 2

        @pl.when(slot < middle)
        def _():
            dispatch(slot, low, middle)

        @pl.when(slot >= middle)
        def _():
            dispatch(slot, middle, high)

    @pl.loop(0, len(SLOTS))
    def _(slot):
        dispatch(slot, 0, len(SLOTS))

    for (kind, role, way), count in sorted(sent.items()):

        @pl.when((row_place if kind == 0 else col_place) == role)
        def _(way=way, count=count):
            block = right.at[pl.ds(0, 8 * reads if way == CORE else count * piece)]
            copy(block, block, way, core_sem).wait_send()
            if way == CORE:
                copy(block, block, way, core_sem).wait_recv()


def gather(tile_pattern, weights):
    reads, bins = weights.shape
    return pl.pallas_call(
        gather_kernel,
        out_shape=(pltpu.VMEM((8 * reads, bins), weights.dtype), pltpu.VMEM((16 * reads, bins), weights.dtype)),
        in_specs=[pl.BlockSpec(memory_space=pltpu.HBM), pl.BlockSpec(memory_space=pltpu.HBM)],
        out_specs=(pl.BlockSpec(memory_space=pltpu.VMEM),) * 2,
        scratch_shapes=[
            pltpu.SMEM(tile_pattern.shape, tile_pattern.dtype),
            pltpu.VMEM(weights.shape, weights.dtype),
            pltpu.SemaphoreType.DMA((2,)),
            pltpu.SemaphoreType.DMA((7,)),
            pltpu.SemaphoreType.DMA((8, CHUNKS)),
            pltpu.SemaphoreType.DMA((8, CHUNKS)),
            pltpu.SemaphoreType.DMA,
        ],
        compiler_params=pltpu.CompilerParams(collective_id=0, has_side_effects=True, vmem_limit_bytes=8 << 20),
        name="gather",
    )(*[pltpu.with_memory_space_constraint(a, pltpu.HBM) for a in (tile_pattern, weights)])


def product_kernel(scale, left, right, out, full, stage, sems):
    row, col = lax.axis_index("row"), lax.axis_index("col")
    slots, _, tile = stage.shape
    section_count = full.shape[1]
    bin_tile = left.shape[1] // section_count
    rows, cols = left.shape[0] // tile, right.shape[0] // tile

    def tile_at(index):
        return pl.ds(pl.multiple_of(index * tile, tile), tile)

    def write(j, slot):
        return pltpu.make_async_copy(stage.at[slot], out.at[:, tile_at(j)], sems.at[slot])

    for j in range(cols):
        for s in range(section_count):
            part = jnp.abs(right[pl.ds(j * tile, tile), pl.ds(s * bin_tile, bin_tile)]).reshape(-1, 16, bin_tile)
            top = jnp.max(jnp.max(part, axis=0).astype(jnp.float32))
            full[j, s] = (top > 0.0).astype(jnp.int32)

    @pl.loop(0, cols)
    def _(j):
        slot = lax.rem(j, slots)

        @pl.when(j >= slots)
        def _():
            write(j - slots, slot).wait()

        case = full[j, 0] + 2 * full[j, 1]

        def put(part):
            stage[slot] = (dot(left[:, part], right[tile_at(j), part]) * scale).astype(stage.dtype)

        @pl.when(case == 0)
        def _():
            stage[slot] = jnp.zeros(stage.shape[1:], stage.dtype)

        @pl.when(case == 1)
        def _():
            put(pl.ds(0, bin_tile))

        @pl.when(case == 2)
        def _():
            put(pl.ds(bin_tile, bin_tile))

        @pl.when(case == 3)
        def _():
            put(pl.ds(0, 2 * bin_tile))

        i = col * cols + j - row * rows

        @pl.when(jnp.logical_and(i >= 0, i < rows))
        def _():
            stage[slot, tile_at(i), :] = clear_diagonal(stage[slot, tile_at(i), :])

        write(j, slot).start()

    for j in range(cols - slots, cols):
        write(j, j % slots).wait()


def product(left, right, section_count):
    rows, cols = left.shape[0], right.shape[0]
    tile = rows // 8
    slots = 8

    def kernel(*refs):
        product_kernel(1.0 / math.sqrt(left.shape[1]), *refs)

    return pl.pallas_call(
        kernel,
        out_shape=jax.ShapeDtypeStruct((rows, cols), left.dtype),
        in_specs=[pl.BlockSpec(memory_space=pltpu.VMEM)] * 2,
        out_specs=pl.BlockSpec(memory_space=pl.ANY),
        scratch_shapes=[
            pltpu.SMEM((cols // tile, section_count), jnp.int32),
            pltpu.VMEM((slots, rows, tile), left.dtype),
            pltpu.SemaphoreType.DMA((slots,)),
        ],
        compiler_params=pltpu.CompilerParams(vmem_limit_bytes=24 << 20),
        name="product",
    )(left, right)


def shards(weights, tile_pattern):
    return product(*gather(tile_pattern, weights), tile_pattern.shape[1])


def solution(mesh):
    return jax.shard_map(
        shards,
        mesh=mesh,
        in_specs=(P(("row", "col"), None), P(("row", "col"), None)),
        out_specs=P("row", "col"),
        check_vma=False,
    )
```

```python
import math

import jax
import jax.numpy as jnp
from jax import lax
from jax.experimental import pallas as pl
from jax.experimental.pallas import tpu as pltpu
from jax.sharding import PartitionSpec as P

MESH = pl.DeviceIdType.MESH
CHUNKS = 8
UNITS = 4
SLOTS = (
    (
        (0,0,((0,0,1,5),(0,1,0,1,4,6),(0,2,1,4),(0,3,0,3,6),(0,4,0,1,4),(0,5,0,3,6),(0,6,1,5),(0,7,0,1,5,6))),
        (0,1,((1,0,0,1),(1,1,0,1,2),(1,2,0,1,2),(1,3,0),(1,4,0,1),(1,5,0,2),(1,6,0,1),(1,7,0,2))),
        (0,2,((2,0,1,2),(2,1,0,2),(2,2,1),(2,3,0,1,2),(2,4,0,2),(2,5,0,1,2),(2,6,1),(2,7,2))),
        (0,3,((3,0,0,2),(3,1,0,1,2),(3,2,2),(3,3,1),(3,4,1),(3,5,0),(3,6,0,2),(3,7,0,1,2))),
        (0,4,((4,0,0,2),(4,1,0,2),(4,2,0,1),(4,3,0,1),(4,4,1,2),(4,5,0,1),(4,6,0,1,2),(4,7,0,1,2))),
        (0,5,((5,0,1,2),(5,1,1),(5,2,0,1),(5,3,0,2),(5,4,0,1),(5,5,2),(5,6,1,2),(5,7,1,2))),
        (0,6,((6,0,0),(6,1,0,2),(6,2,1,2),(6,3,0,2),(6,4,1,2),(6,5,0),(6,6,0,2),(6,7,1,2))),
        (0,7,((7,0,1),(7,1,0,1),(7,2,0,1,2),(7,3,0,1),(7,4,2),(7,5,1),(7,6,1),(7,7,0,1,2))),
    ),
    (),
    (),
    (),
    (),
    (),
    (),
    (),
    (),
    (),
    (),
    (
        (1,4,((0,0,3),)),
        (0,0,((3,0,0,4),(1,0,1,3))),
        (0,1,((2,0),(0,1))),
        (0,2,((1,0,2),(3,1,2))),
        (0,3,((0,0,1),(2,1,0))),
        (0,4,((5,0,1),(7,1,0,2))),
        (0,5,((4,0,0,2),)),
        (0,6,((7,0,1,2),)),
        (0,7,((6,0,0),)),
    ),
    (
        (1,3,((0,1,4),)),
        (0,5,((6,2,1),)),
        (0,6,((5,2),)),
        (0,7,((4,2,1,2),)),
    ),
    (
        (1,1,((0,3,3),)),
        (0,0,((4,0,1,3,5),)),
        (0,1,((5,0,0,1),)),
        (0,6,((2,0,1),)),
        (0,7,((3,0,0),)),
    ),
    (
        (0,2,((6,1,0),)),
        (0,3,((7,2,1),)),
        (0,5,((1,1,0),)),
    ),
    (
        (1,4,((0,6,3,4),)),
        (0,0,((3,1,4,6),(1,1,5,6))),
        (0,1,((2,2,1,2),)),
        (0,2,((1,1,0),)),
        (0,3,((0,1,1),)),
        (0,4,((5,1,1,2),)),
        (0,5,((4,1,0),)),
        (0,6,((7,1),)),
        (0,7,((6,1,0),)),
    ),
    (
        (1,3,((0,2,4,5),)),
        (0,1,((0,3,0),)),
        (0,2,((3,3,1,2),)),
        (0,3,((2,3,0),)),
        (0,4,((7,2,0),)),
        (0,5,((6,4,1,2),)),
        (0,6,((5,3,0),)),
        (0,7,((4,3,2),)),
    ),
    (),
    (
        (1,1,((0,5,3,5),)),
        (0,0,((4,1,1,3,6),)),
        (0,1,((5,3,0),)),
        (0,2,((6,2,1),)),
        (0,5,((1,2,0),)),
        (0,6,((2,1,1),)),
        (0,7,((3,1),)),
    ),
    (
        (0,3,((7,4,0,1),)),
    ),
    (
        (1,4,((0,7,3,4,6),)),
        (0,0,((3,5,0,5),(1,2,1,5))),
        (0,1,((2,3),(0,4))),
        (0,2,((1,2),(3,4,1,2))),
        (0,3,((0,2,1),(2,4,0))),
        (0,4,((5,2,1),(7,3,0))),
        (0,5,((4,2),)),
        (0,6,((7,2),)),
        (0,7,((6,3,0),)),
    ),
    (
        (1,3,((0,4,4),)),
        (0,5,((6,7,1),)),
        (0,6,((5,4),)),
        (0,7,((4,4,1),)),
    ),
    (
        (0,0,((4,4,1,3),)),
        (0,1,((5,5,0),)),
        (0,6,((2,3,1),)),
        (0,7,((3,2,0,1),)),
    ),
    (
        (1,1,((1,0,3),)),
        (1,2,((0,1,4,5),)),
        (1,5,((0,0,5,3),)),
        (0,2,((6,3,1),)),
        (0,3,((7,7,0,1),)),
        (0,5,((1,5,1),)),
    ),
    (
        (1,2,((0,3,3,5),)),
        (0,0,((3,6,5),(1,4,1,4))),
        (0,1,((2,5),)),
        (0,2,((1,3,0,2),)),
        (0,3,((0,4,1,2),)),
        (0,4,((5,4,2),)),
        (0,5,((4,3,0,2),)),
        (0,6,((7,3,2),)),
        (0,7,((6,5,0,2),)),
    ),
    (
        (1,3,((3,0,4,5),)),
        (1,4,((4,0,3,4),)),
        (0,1,((0,5,0),)),
        (0,2,((3,7,1),)),
        (0,3,((2,5,0),)),
        (0,4,((7,7,0),)),
        (0,5,((7,0,1),)),
        (0,6,((4,0,0),)),
        (0,7,((4,5),)),
    ),
    (),
    (
        (1,1,((4,0,3),)),
        (1,5,((0,6),)),
        (1,7,((0,6,5,4),)),
        (0,0,((4,6,0,4),)),
        (0,1,((5,6,0,1),)),
        (0,2,((6,4),)),
        (0,5,((1,7,1),)),
        (0,6,((2,4,0),)),
        (0,7,((3,6,0,1),)),
    ),
    (
        (1,2,((0,2,4,6),)),
        (0,3,((4,2,0,1),)),
    ),
    (
        (1,2,((0,5,3),)),
        (1,4,((1,1,3,4),)),
        (0,0,((3,7,5,6),(1,6,3))),
        (0,1,((2,6,1,2),(0,7))),
        (0,2,((1,4,2),(0,0,1,2))),
        (0,3,((0,6,1,2),(6,1,0))),
        (0,4,((5,6,1),(6,0,0,2))),
        (0,5,((4,5,0,2),)),
        (0,6,((7,5,2),)),
        (0,7,((6,6,0),)),
    ),
    (
        (1,3,((3,1,4,5,6),)),
        (0,5,((2,0,1),)),
        (0,6,((1,1,0),)),
        (0,7,((4,6,1,2),)),
    ),
    (
        (0,0,((4,7,0,1,3,6),)),
        (0,1,((5,7,0,1),)),
        (0,6,((2,5,0),)),
        (0,7,((3,7,1),)),
    ),
    (
        (1,1,((4,1,3,6),)),
        (1,2,((0,4,4,5,6),)),
        (1,5,((0,7,5,3,6),)),
        (1,7,((0,7,6),)),
        (0,2,((6,6,0),)),
        (0,3,((4,3,1),)),
        (0,5,((2,2,0,1),)),
    ),
    (
        (0,0,((2,1,0,4),(5,0,1,4))),
        (0,1,((3,3,1,2),)),
        (0,2,((1,5,0),)),
        (0,3,((0,7,1,2),)),
        (0,4,((5,7,1),)),
        (0,5,((4,6),)),
        (0,6,((7,6,1,2),)),
        (0,7,((5,3,0),)),
    ),
    (
        (1,2,((1,0,3,5),)),
        (1,4,((3,5,3,4),)),
        (1,6,((0,0,3),)),
        (0,1,((3,0,0),)),
        (0,2,((7,2,1),)),
        (0,3,((1,1),)),
        (0,4,((3,0,0),)),
        (0,5,((2,1,1),)),
        (0,6,((4,1,0),)),
        (0,7,((4,7),)),
    ),
    (
        (1,1,((0,1),)),
        (1,6,((0,1,4,3,6),)),
    ),
    (
        (1,1,((4,4,3,5),)),
        (1,3,((1,4,4,5),)),
        (0,0,((7,1,4),)),
        (0,1,((4,0,0),)),
        (0,2,((6,7,0,1),)),
        (0,6,((2,7,0),)),
    ),
    (
        (1,2,((3,0,4),)),
        (1,3,((0,3,6),)),
        (1,5,((4,0),)),
        (1,7,((4,0,4),)),
    ),
    (
        (1,2,((4,0,3),)),
        (1,4,((1,2,3,4),)),
        (0,0,((2,3,4,5),(2,2,1,3,6))),
        (0,1,((6,2,1),(3,5,0,2))),
        (0,2,((1,6,0,2),(0,1,2))),
        (0,3,((1,0),(1,3,0))),
        (0,4,((6,2,1),(6,1,0))),
        (0,5,((4,7,0),)),
        (0,6,((7,7),)),
        (0,7,((4,0),)),
    ),
    (
        (1,6,((0,6,5),)),
        (0,5,((2,3,1),)),
        (0,6,((1,2,0),)),
        (0,7,((5,0),)),
    ),
    (
        (1,5,((0,5,4,3),)),
        (1,7,((0,2,3,4),)),
        (0,0,((5,1,0,1,5,6),)),
        (0,1,((6,4,1),)),
        (0,3,((6,5,1,0),)),
        (0,6,((1,0,1,0),)),
        (0,7,((0,4,0),)),
    ),
    (
        (1,1,((0,0,3,6),(0,2,6),(1,6,3,5))),
        (1,2,((3,1,4,6),)),
        (1,3,((4,6,4),(0,5,6))),
        (1,5,((1,1,5),)),
        (1,7,((1,1,4),)),
        (0,2,((7,0,0,1),)),
    ),
    (
        (1,6,((0,3,4,3),)),
        (0,0,((7,4,0,3),(5,6,1,5))),
        (0,1,((3,4,1),)),
        (0,2,((1,7),)),
        (0,3,((4,0),)),
        (0,4,((6,4,1),)),
        (0,5,((7,1,2),)),
        (0,6,((4,2),)),
        (0,7,((2,4,0),)),
    ),
    (
        (1,4,((3,6,3,4),)),
        (0,1,((4,6,0),)),
        (0,2,((7,4),)),
        (0,3,((6,6,0),)),
        (0,4,((6,3,0),)),
        (0,6,((4,3),)),
        (0,7,((5,1,1),)),
    ),
    (
        (0,5,((2,6,0,1),(7,6,1))),
    ),
    (
        (1,1,((0,4,6),(4,7,3,5))),
        (1,2,((4,1,3,5,6),)),
        (1,3,((2,1,4),(0,6))),
        (1,6,((0,7,5,6),)),
        (1,7,((0,0),)),
        (0,6,((3,1,1),)),
    ),
    (
        (1,3,((1,0),)),
        (1,5,((3,5,5),(0,1,6))),
        (1,7,((3,5,5,4),)),
    ),
    (
        (1,2,((1,4),)),
        (1,4,((3,7,3,4,6),)),
        (0,0,((2,4,0,5),(2,6,1,3,4))),
        (0,1,((6,3,1),(4,7))),
        (0,2,((5,0,2),(7,3,0,1),(0,2,1,2))),
        (0,3,((4,1,1),(4,6),(1,5,2))),
        (0,4,((6,7,1),(3,2,2,0))),
        (0,5,((7,2),)),
        (0,6,((4,4,1),)),
        (0,7,((1,1,0),(0,6,0,1))),
    ),
    (
        (1,6,((4,0),)),
        (0,1,((4,3,1),)),
        (0,5,((3,3,1),)),
        (0,6,((4,5),)),
        (0,7,((5,2,2),)),
    ),
    (
        (1,2,((4,4,3),)),
        (1,7,((3,0,3,4),)),
        (0,0,((5,4,0,1,4,5),)),
        (0,6,((3,3),)),
    ),
    (
        (1,1,((2,2,5),(3,0))),
        (1,3,((5,0,4),(4,0))),
        (1,5,((1,2,3),)),
        (1,7,((0,1,3,6),(1,2,5))),
    ),
    (
        (0,0,((7,7,0,3),(5,7,4,6))),
        (0,1,((3,7),)),
        (0,2,((0,3,0,2),)),
        (0,3,((1,2),)),
        (0,4,((1,5,2),)),
        (0,5,((7,3),(1,0))),
        (0,6,((3,2,2),)),
        (0,7,((2,5,0),(0,7,1))),
    ),
    (
        (1,2,((0,6,4),(4,6,5))),
        (1,4,((2,3,4),)),
        (0,1,((2,1),)),
        (0,2,((7,7),)),
        (0,3,((6,7),)),
        (0,4,((6,5,0),)),
        (0,6,((2,2,0),)),
        (0,7,((5,6,1),)),
    ),
    (
        (1,4,((0,2,3),(0,5))),
        (1,6,((0,5,3),(0,2,6))),
    ),
    (
        (1,1,((3,1,6),(7,4,3,5))),
        (1,2,((0,0,3,6),)),
        (1,3,((7,1,4,5),)),
        (1,5,((4,4,3),)),
        (0,2,((7,5,0,1),)),
        (0,6,((3,4,1),)),
    ),
    (
        (1,5,((3,6,3),(0,3,4))),
        (1,6,((0,4,4,3,6),)),
        (1,7,((3,6),(0,3,6))),
        (0,1,((4,5,1,0),)),
    ),
    (
        (1,1,((0,7),)),
        (1,3,((4,1,6),)),
        (1,4,((5,1,3,4),)),
        (0,0,((2,5,5,6),(3,3,3),(6,0,1,0,5))),
        (0,1,((0,0,2),(5,1))),
        (0,2,((5,3,0),(0,4))),
        (0,3,((4,4,1),(1,6))),
        (0,4,((7,0),(3,6))),
        (0,5,((7,7),(3,1,2,1))),
        (0,6,((3,6,2,1),)),
        (0,7,((4,1),)),
    ),
    (
        (1,2,((2,1,4,5),(0,7,3,6))),
        (0,6,((4,7),)),
        (0,7,((5,7),)),
    ),
    (
        (1,2,((1,6,3),)),
        (1,6,((1,1,5),)),
        (1,7,((3,1,3,4,6),)),
        (0,5,((3,5,1,0),)),
        (0,6,((1,3,1,0),)),
    ),
    (
        (1,1,((2,6,3),)),
        (1,3,((2,3,4),)),
        (1,5,((1,6,4,3),)),
        (0,2,((7,6,0,1),)),
    ),
    (
        (1,3,((3,5,4),)),
        (1,5,((3,7,5,6),)),
        (1,6,((1,0,4,3,6),)),
        (0,0,((4,2,3,5),(6,2,4))),
        (0,1,((7,2,1),)),
        (0,2,((5,5,2,0),)),
        (0,3,((1,4),)),
        (0,4,((1,7,1),)),
        (0,5,((6,0),(4,4))),
        (0,6,((4,6),)),
        (0,7,((2,7,2,0),)),
    ),
    (
        (1,1,((1,1,6),)),
        (1,3,((4,4),)),
        (1,4,((5,6,3,4),)),
        (1,7,((3,7,5,4,6),)),
        (0,1,((7,4,2),)),
        (0,2,((4,2,1),)),
        (0,3,((7,0,0),)),
        (0,4,((6,6,0),)),
        (0,6,((2,6,0),)),
        (0,7,((6,2,2),)),
    ),
    (
        (1,2,((5,0,4,5),)),
        (1,4,((3,0),)),
        (1,6,((3,5),)),
    ),
    (
        (1,1,((7,7,3,5),)),
        (1,2,((4,7,3,6),)),
        (1,3,((2,6,5),)),
        (1,6,((1,2,5),)),
        (1,7,((1,4,3,4),)),
        (0,6,((1,4,1,0),)),
    ),
    (
        (1,1,((0,6,6),)),
        (1,7,((0,5),)),
    ),
    (
        (1,4,((2,4,3,4),)),
        (1,5,((4,7,4,3),(0,2,6))),
        (1,7,((2,3,4),)),
        (0,0,((6,1,0,3,6),(6,4,1,5))),
        (0,1,((6,7,1),(2,4))),
        (0,2,((0,5,0,2),(0,6,1))),
        (0,3,((4,7,1),(7,3))),
        (0,4,((2,0,2,1),(5,3))),
        (0,5,((3,0),(3,4,1))),
        (0,6,((3,7,1),)),
        (0,7,((1,2,0),)),
    ),
    (
        (1,2,((7,1,4,5),)),
        (1,4,((0,1,6),)),
        (1,6,((4,1,4,3,6),)),
        (0,1,((7,1,0),)),
        (0,3,((5,2,1,0),)),
        (0,7,((6,4),)),
    ),
    (
        (1,1,((3,5),)),
        (1,3,((0,0,6),)),
        (1,4,((0,3,6),)),
        (1,5,((0,4,4,6),)),
        (1,6,((3,0,4),(4,4,3))),
        (0,6,((0,0,0),)),
    ),
    (
        (1,1,((3,3,3,5),)),
        (1,2,((7,4),)),
        (1,3,((5,4,4),(1,2))),
        (0,7,((1,5,1),)),
    ),
    (
        (1,7,((0,4,6),)),
        (0,0,((1,3,3,6),(3,4,4,6))),
        (0,1,((7,0),)),
        (0,2,((5,6),)),
        (0,3,((5,0),)),
        (0,4,((2,2),)),
        (0,5,((6,1),(3,6,2))),
        (0,6,((5,1),)),
        (0,7,((1,0,0),)),
    ),
    (
        (1,1,((2,1),)),
        (1,4,((5,4,4),)),
        (1,5,((5,1,5),)),
        (1,7,((5,1,4),)),
        (0,1,((5,4),)),
        (0,2,((4,3),)),
        (0,3,((0,3,2),)),
        (0,4,((0,4,0),)),
        (0,7,((6,7),)),
    ),
    (
        (1,4,((3,1,3,6),)),
        (1,6,((3,1,6),)),
    ),
    (
        (1,1,((4,2,3),)),
        (1,2,((2,3,4),(1,1,3,6))),
        (1,3,((0,7,6),(5,7,4))),
        (1,4,((1,6),)),
        (1,6,((3,6,5),)),
        (0,0,((3,2,0,4,6),)),
        (0,2,((3,2),)),
        (0,6,((3,5),(1,6,1,0))),
    ),
    (
        (1,2,((2,6),)),
        (1,5,((1,0,6),)),
        (1,6,((4,6,4,3),)),
    ),
    (
        (1,1,((5,0),)),
        (1,4,((2,5,3,4,6),)),
        (1,5,((5,6,5,3),)),
        (1,7,((1,0,3,6),(5,6,5))),
        (0,0,((6,5,0,3,6),(6,3,1,3,6))),
        (0,1,((7,3,1),(7,7))),
        (0,2,((5,7,2,0),(0,7))),
        (0,3,((2,2),(7,5))),
        (0,4,((2,1,1),(2,4,0))),
        (0,5,((6,3),(1,3))),
        (0,6,((0,6),)),
        (0,7,((2,2),)),
    ),
    (
        (1,4,((1,4),)),
        (1,5,((2,2,4,3),)),
        (1,7,((7,1,3),)),
        (0,5,((0,0),)),
        (0,7,((1,7,2,1),)),
    ),
    (
        (1,2,((3,5),)),
        (1,3,((1,6),)),
        (1,6,((3,7,5,6),(1,6,3))),
        (0,0,((1,5,5,6),)),
        (0,3,((2,7,0),)),
        (0,6,((0,1,1,0),)),
    ),
    (
        (1,1,((6,1,3,5),)),
        (1,3,((6,2,4,5),)),
    ),
    (
        (1,2,((7,7,3),)),
        (1,3,((3,7),)),
        (1,4,((4,7),)),
        (1,5,((4,1,4,6),)),
        (1,7,((4,1,6),)),
        (0,0,((6,6,0,3),(4,3,4,6))),
        (0,1,((0,2),(3,1))),
        (0,2,((3,0,2),)),
        (0,3,((5,1,1),)),
        (0,4,((2,3,1),)),
        (0,5,((3,2),(1,4))),
        (0,6,((0,7,1),)),
        (0,7,((1,3,0),)),
    ),
    (
        (1,2,((1,2,4),)),
        (1,4,((6,0,3,4),)),
        (1,5,((2,4,5,3),(7,4,4,3))),
        (1,7,((2,4,5),)),
        (0,1,((6,0,0),)),
        (0,2,((3,6),(6,5))),
        (0,3,((5,3,0),)),
        (0,4,((1,1),)),
        (0,7,((2,0),)),
    ),
    (
        (1,1,((7,1),)),
        (1,6,((2,1,4,3),(1,4,4))),
        (0,3,((6,2),)),
    ),
    (
        (1,1,((1,3,3,5),(3,7))),
        (1,3,((4,7,6),(3,4,4,5,6))),
        (1,6,((4,7,3,6),)),
        (0,6,((5,0),)),
    ),
    (
        (1,4,((0,4,6),)),
        (1,5,((3,0),)),
        (1,7,((2,6,3,4),)),
    ),
    (
        (1,2,((5,4,4),(3,3,3))),
        (1,4,((4,2,3,4),)),
        (1,5,((3,1,6),)),
        (1,7,((4,4,3),(5,4,4))),
        (0,0,((7,0,5,6),(4,5,4,6))),
        (0,1,((7,5,2,1),(6,1))),
        (0,2,((4,0),(4,1,1))),
        (0,3,((5,6),(7,6))),
        (0,4,((2,6),(0,6,0))),
        (0,5,((6,5),(3,7,1))),
        (0,6,((5,6),)),
        (0,7,((2,6),)),
    ),
    (
        (0,5,((7,4,1,0),)),
    ),
    (
        (1,1,((2,3,6),)),
        (1,6,((2,3,4),)),
        (0,6,((0,2,1,0),)),
    ),
    (
        (1,1,((6,5,3,5),)),
        (1,3,((3,2,4,5),(1,1,6))),
        (1,4,((1,0,6),)),
        (1,6,((5,6,5),)),
        (0,7,((2,1),)),
    ),
    (
        (1,1,((5,1,6),)),
        (1,2,((3,6,4,3),(5,7,5))),
        (1,5,((4,6,5,6),(7,7,4,3))),
        (1,6,((5,0,4,3),)),
        (1,7,((4,6,3),)),
        (0,0,((5,2,0,3),(7,2,4))),
        (0,1,((7,6,1),)),
        (0,2,((3,5),)),
        (0,3,((2,6),)),
        (0,4,((7,6),)),
        (0,5,((6,6),(1,6))),
        (0,6,((1,5),)),
        (0,7,((1,4,0),)),
    ),
    (
        (1,2,((4,2,5),)),
        (1,3,((5,6,6),)),
        (1,4,((6,4,3,4),)),
        (1,5,((2,5,5,6),)),
        (1,7,((2,5,5,4,6),)),
        (0,1,((3,2),(3,6))),
        (0,2,((4,4,1),)),
        (0,3,((5,5,0),)),
        (0,4,((2,5,0),)),
    ),
    (
        (1,4,((2,2,6),)),
        (1,6,((5,1,5,6),)),
    ),
    (
        (1,1,((6,3,3,5),)),
        (1,3,((4,3,4,5),)),
        (1,4,((7,1),)),
        (0,6,((0,3,1),)),
        (0,7,((0,3),(2,3))),
    ),
    (
        (1,2,((3,7,6),)),
        (1,5,((2,1,4),)),
        (1,6,((2,2,5,3,6),(7,1,4))),
    ),
    (
        (1,2,((6,2,4,5),(6,1,3))),
        (1,3,((2,4),)),
        (1,4,((1,5,3,4,6),)),
        (1,5,((6,0,5),)),
        (1,7,((6,2),(1,6),(6,0,5,4))),
        (0,0,((2,7,0,3,5,6),(6,7,4,5,6),(2,0,1,3,5,6))),
        (0,1,((4,2),(6,5))),
        (0,2,((4,6),(4,7))),
        (0,3,((5,4,2,1),(1,7,0),(0,5))),
        (0,4,((3,3,1),(2,7,0))),
        (0,5,((0,4,0),(0,1))),
        (0,6,((1,7),)),
        (0,7,((0,0,0),)),
    ),
    (
        (1,1,((5,6),)),
        (1,3,((7,7),)),
    ),
    (
        (1,6,((2,6),)),
        (0,6,((5,5,0),)),
    ),
    (
        (1,1,((6,6,3,5),(1,2,6))),
        (1,3,((4,5,4,5,6),)),
        (1,4,((4,1,6),(2,6,3))),
        (1,5,((3,3,4,3),)),
        (1,6,((2,4,5),)),
    ),
    (
        (1,2,((3,4,4,5,6),)),
        (1,5,((1,4,5),)),
        (1,7,((3,4,3,6),(2,1))),
        (0,0,((5,3,3,5,6),(7,3,4,5,6))),
        (0,1,((0,6),)),
        (0,2,((4,5,0),)),
        (0,3,((6,0),)),
        (0,4,((3,1),)),
        (0,5,((2,4),(0,7,1))),
        (0,7,((1,6,0),)),
    ),
    (
        (1,1,((2,4),)),
        (1,2,((1,3,3,6),)),
        (1,4,((7,0,3,4,6),(7,4))),
        (1,5,((4,2),)),
        (1,7,((4,2,5),)),
        (0,1,((6,6),)),
        (0,2,((5,2),)),
        (0,3,((5,7),)),
        (0,4,((1,2),)),
        (0,6,((7,4),)),
    ),
    (
        (1,3,((3,3,6),)),
    ),
    (
        (1,1,((5,2,3,5),(5,4))),
        (1,3,((7,2,4,5),)),
        (1,4,((4,4),)),
        (1,6,((5,4,4),)),
        (0,6,((0,5,1,0),)),
    ),
    (
        (1,3,((2,5,6),)),
        (1,5,((2,3,6),)),
        (1,6,((7,4,3),)),
        (0,5,((7,5,1),)),
    ),
    (
        (1,2,((3,2,4,6),(6,5,3))),
        (1,5,((6,1,3,6),(6,4,5))),
        (1,7,((3,2,3,4),(4,7,6),(6,4,5))),
        (0,0,((5,5,3,5,6),(7,5,3,4,5,6))),
        (0,1,((4,1),(5,2))),
        (0,2,((7,1,0),(5,1))),
        (0,3,((6,4),)),
        (0,4,((3,5,1),(1,0))),
        (0,5,((0,6),(0,2,1))),
        (0,7,((0,1,0),)),
    ),
    (
        (1,1,((4,6,6),)),
        (1,6,((5,7,4,3,6),)),
    ),
    (
        (1,2,((5,6,6),)),
        (1,3,((3,6,6),)),
        (1,4,((7,7,4),)),
        (1,6,((2,5,5,6),)),
        (0,6,((0,4),(5,7))),
        (0,7,((3,3),)),
    ),
    (
        (1,1,((3,6,6),)),
        (1,3,((6,7,4,5),(6,0))),
        (1,4,((4,6,6),)),
        (1,6,((7,7),)),
    ),
    (
        (1,1,((2,7,3,6),)),
        (1,2,((5,1,3,6),(4,3,4,6))),
        (1,4,((2,7,3,4,6),)),
        (1,5,((5,0,6),(1,3,4,3,6))),
        (1,6,((4,2),)),
        (1,7,((5,0,3,6),)),
        (0,0,((7,6,3,4,5,6),)),
        (0,1,((4,4),)),
        (0,2,((6,0),)),
        (0,3,((6,3),)),
        (0,4,((3,4,1),)),
        (0,5,((2,5),(0,3,1))),
        (0,7,((0,2),)),
    ),
    (
        (1,1,((2,5,6),)),
        (1,2,((6,3,3,5,6),)),
        (1,5,((1,5,5,3,6),)),
        (1,7,((1,5,5,6),(4,3,3,4,6))),
        (0,0,((1,7,3,4,5,6),)),
        (0,1,((2,7),)),
        (0,2,((5,4),)),
        (0,4,((1,3),)),
    ),
    (
        (1,1,((2,0,3,6),)),
        (1,2,((2,2,6),)),
        (1,4,((6,7,3),(2,1))),
    ),
    (
        (1,3,((7,3,4,5,6),(6,1,6))),
        (1,4,((3,4,6),)),
        (1,6,((6,0,5),)),
        (0,3,((4,5),)),
        (0,6,((3,0),)),
    ),
    (
        (1,1,((6,2,6),)),
        (1,3,((4,2,6),)),
        (1,5,((7,1),)),
        (1,6,((3,3,3),)),
    ),
    (
        (1,2,((4,5,4,6),(6,6,3))),
        (1,5,((6,5,4,3,6),(2,6))),
        (1,7,((2,2,5,6),(4,5,3,4,6))),
        (0,3,((2,0),)),
        (0,4,((1,4),)),
        (0,5,((2,7),(0,5))),
        (0,7,((5,5,0),)),
    ),
    (
        (1,1,((6,0,6),)),
        (1,4,((2,0,3,4,6),)),
        (1,7,((7,0,5,4,6),)),
        (0,4,((3,7),)),
    ),
    (
        (1,4,((3,3),)),
        (1,6,((3,2,4,6),)),
        (0,7,((3,5),)),
    ),
    (
        (1,1,((5,3,3,5,6),(3,4,6))),
        (1,3,((7,5),(1,3,6))),
        (1,4,((3,2,6),)),
        (1,6,((6,2,4),(6,1,3,6))),
        (0,3,((7,1),)),
        (0,4,((7,4),)),
        (0,7,((5,4),)),
    ),
    (
        (1,2,((7,2,4),)),
        (1,3,((6,4,4),)),
        (1,5,((5,4),(6,3,4))),
        (1,7,((7,4,5),)),
        (0,7,((0,5,0),)),
    ),
    (
        (1,1,((1,4),)),
        (1,2,((5,2,3,5),)),
        (1,5,((7,0,5,6),)),
        (1,7,((7,2,3,4),)),
        (0,4,((0,0),)),
    ),
    (
        (1,2,((2,4),)),
        (1,7,((7,7),)),
    ),
    (
        (1,3,((7,6,4,5,6),(6,5,6))),
        (1,4,((1,3,4,6),)),
        (1,6,((3,4,4,6),)),
        (0,7,((3,4),)),
    ),
    (
        (1,1,((3,2,6),(5,5,3,6))),
        (1,3,((1,5,6),)),
        (1,4,((5,3,4),)),
        (1,6,((1,3,6),(4,3,4,6))),
    ),
    (
        (1,2,((6,7,4,6),)),
        (1,4,((5,0,6),)),
        (1,5,((5,7,5,6),(6,6,4,3),(6,7,6))),
        (1,7,((5,7,3,6),(6,7,4))),
        (0,4,((0,7),(1,6))),
    ),
    (
        (1,1,((6,4,6),)),
        (1,4,((7,3,3),)),
    ),
    (
        (1,1,((7,5,3,6),)),
        (1,2,((2,5,6),)),
        (1,4,((4,3,6),(6,5,6))),
    ),
    (
        (1,1,((4,3,6),)),
        (1,2,((2,7,3,6),(2,0,5,6))),
        (1,3,((1,7,4,5,6),(5,1,6))),
        (1,6,((6,3,3,6),(1,5,5,6))),
    ),
    (
        (1,2,((7,3,4,6),)),
        (1,3,((2,2,6),)),
        (1,5,((5,2,4),)),
        (1,6,((4,5,6),)),
        (1,7,((2,7,6),(2,0,5,6))),
        (0,4,((7,5),)),
    ),
    (
        (1,1,((1,5,6),)),
        (1,7,((3,3,6),(7,3,6))),
        (0,4,((0,1),)),
    ),
    (
        (1,2,((6,0,6),)),
        (1,5,((3,2,6),)),
    ),
    (
        (1,1,((7,6,5,6),)),
        (1,3,((6,3,6),)),
        (1,4,((6,3),)),
        (1,5,((2,7,3,6),(2,0,6))),
    ),
    (
        (1,1,((4,5,5,6),)),
        (1,3,((7,0,6),)),
        (1,4,((4,5,6),(5,5,3,4,6))),
        (1,5,((6,2,4,6),)),
        (1,6,((7,0,5,6),(6,5,3))),
    ),
    (
        (1,2,((6,4,5,6),)),
        (1,5,((5,3,3,6),)),
        (1,6,((5,2),)),
        (1,7,((6,1,3,6),)),
        (0,4,((0,2),(5,5))),
    ),
    (
        (1,1,((7,0,6),)),
        (1,2,((5,3,6),)),
        (1,4,((7,5,3,4,6),)),
        (1,7,((7,6,4,6),)),
    ),
    (
        (1,7,((1,3,6),)),
    ),
    (
        (1,1,((1,7,5,6),(7,2))),
        (1,3,((6,6,6),)),
        (1,4,((7,2,6),(6,6,6))),
    ),
    (
        (1,3,((7,4,6),)),
        (1,6,((6,6,3),(7,2,4))),
        (0,4,((0,3),)),
    ),
    (
        (1,1,((5,7,6),)),
        (1,2,((7,6,6),)),
        (1,5,((7,3,3),(3,4,6))),
        (1,7,((6,3,6),)),
        (0,4,((0,5),)),
    ),
    (
        (1,6,((2,0,6),)),
        (1,7,((1,7,4,6),(5,3,5))),
    ),
    (
        (1,2,((1,5,6),(5,5,3,5,6))),
        (1,3,((5,2,5),)),
        (1,4,((7,6,6),)),
    ),
    (
        (1,1,((6,7,6),)),
        (1,2,((7,5,5,6),)),
        (1,3,((2,0,6),)),
        (1,4,((5,7,6),(5,2,6))),
        (1,6,((6,7,6),)),
    ),
    (
        (1,2,((1,7,6),)),
        (1,5,((4,3,6),)),
    ),
    (),
    (
        (1,2,((7,0,6),)),
        (1,4,((1,7,6),)),
        (1,7,((6,5,6),)),
    ),
    (
        (1,1,((7,3,6),)),
        (1,3,((2,7,6),)),
        (1,4,((6,1,6),)),
        (1,5,((7,6,6),(4,5,6))),
    ),
    (
        (1,4,((6,2,6),)),
        (1,5,((5,5,6),(7,5,6))),
        (1,6,((6,4,6),)),
        (1,7,((5,5,6),)),
    ),
    (
        (1,6,((7,6,6),)),
        (1,7,((7,5,6),)),
    ),
    (
        (1,5,((7,2,6),)),
        (1,6,((2,7,6),(5,3,6))),
    ),
    (
        (1,7,((6,6,6),)),
    ),
    (),
    (
        (1,3,((5,3,6),)),
        (1,6,((1,7,6),)),
    ),
    (
        (1,5,((1,7,6),)),
        (1,6,((7,5,6),)),
        (1,7,((5,2,6),)),
    ),
    (),
    (),
    (
        (1,3,((5,5,6),)),
        (1,6,((7,3,6),)),
    ),
    (),
    (
        (1,6,((5,5,6),)),
    ),
)
XP, XM, ZH, YP, YM, ZL, CORE = range(7)


def place():
    row, col = lax.axis_index("row"), lax.axis_index("col")
    return col // 2, lax.rem(col, 2), lax.rem(row // 2, 4), row // 8, lax.rem(row, 2)


def device(x, zh, y, zl, core):
    return (zl * 8 + y * 2 + core, x * 2 + zh)


def neighbours(x, zh, y, zl, core):
    def turn(a, by):
        return lax.rem(a + by, 4)

    return {
        XP: device(turn(x, 1), zh, y, zl, core),
        XM: device(turn(x, 3), zh, y, zl, core),
        ZH: device(x, 1 - zh, y, zl, core),
        YP: device(x, zh, turn(y, 1), zl, core),
        YM: device(x, zh, turn(y, 3), zl, core),
        ZL: device(x, zh, y, 1 - zl, core),
        CORE: device(x, zh, y, zl, 1 - core),
    }


def flip(a, b):
    return a + b - 2 * a * b


class Place:
    def __init__(self):
        self.coordinates = x, zh, y, zl, core = place()
        self.core = core
        self.row_root = (2 * zl + y // 2, lax.rem(y, 2))
        self.col_root = (2 * lax.rem(x, 2) + zh, x // 2)
        self.row_place = lax.rem(x - self.row_root[0] + 4, 4) + 4 * flip(zh, self.row_root[1])
        self.col_place = lax.rem(y - self.col_root[0] + 4, 4) + 4 * flip(zl, self.col_root[1])

    def row_shard(self, source):
        return lax.rem(self.row_root[0] + source % 4, 4) * 2 + flip(self.row_root[1], source // 4)

    def col_shard(self, source):
        return lax.rem(self.coordinates[0] + source % 4, 4) * 2 + flip(self.coordinates[1], source // 4)


def dot(lhs, rhs):
    return lax.dot_general(lhs, rhs, (((1,), (1,)), ((), ())), preferred_element_type=jnp.float32)


def clear_diagonal(block):
    same = lax.broadcasted_iota(jnp.int32, block.shape, 0) == lax.broadcasted_iota(jnp.int32, block.shape, 1)
    return jnp.where(same, 0.0, block.astype(jnp.float32)).astype(block.dtype)


def gather_kernel(
    pattern_hbm, weights_hbm, left, right, pattern_ref, weights_ref, in_sems, send_sems, row_sems, col_sems, core_sem
):
    loads = [
        pltpu.make_async_copy(weights_hbm, weights_ref, in_sems.at[0]),
        pltpu.make_async_copy(pattern_hbm, pattern_ref, in_sems.at[1]),
    ]
    for load in loads:
        load.start()
    reads, bins = weights_ref.shape
    section_count = pattern_ref.shape[1]
    bin_tile = bins // section_count
    piece = reads // CHUNKS
    x, zh, y, zl, core = place()
    near = neighbours(x, zh, y, zl, core)
    barrier = pltpu.get_barrier_semaphore()
    for target in near.values():
        pl.semaphore_signal(barrier, inc=1, device_id=target, device_id_type=MESH)
    own = pl.multiple_of((x * 2 + zh) * reads, reads)
    for load in loads:
        load.wait()
    for section in range(section_count):
        part = pl.ds(section * bin_tile, bin_tile)
        keep = pattern_ref[0, section].astype(jnp.float32)
        left[pl.ds(own, reads), part] = (weights_ref[:, part].astype(jnp.float32) * keep).astype(left.dtype)
    pl.semaphore_wait(barrier, len(near))

    here = Place()
    row_place, col_place = here.row_place, here.col_place
    row_source = [here.row_shard(s) for s in range(8)]
    col_source = [here.col_shard(s) for s in range(8)]
    row_tile = [pl.multiple_of(a * reads, reads) for a in row_source]
    col_tile = [pl.multiple_of((core * 8 + a) * reads, reads) for a in col_source]

    def in_left(s, c):
        return left.at[pl.ds(row_tile[s] + c * piece, piece)]

    def in_right(s, c):
        return right.at[pl.ds(col_tile[s] + c * piece, piece)]

    def copy(src, dst, way, recv_sem):
        return pltpu.make_async_remote_copy(
            src_ref=src, dst_ref=dst, send_sem=send_sems.at[way], recv_sem=recv_sem, device_id=near[way], device_id_type=MESH
        )

    def handle(kind, role, s, c, ways):
        row_sem = row_sems.at[row_source[s], c]
        col_sem = col_sems.at[col_source[s], c]
        if kind == 0:
            src = in_left(s, c)
            if s != role:
                copy(src, src, XP, row_sem).wait_recv()
        else:
            src = in_right(s, c)
            copy(src, src, YP, col_sem).wait_recv()
        for way in ways:
            if way <= ZH:
                copy(src, src, way, row_sem).start()
            elif way <= ZL:
                copy(src, in_right(s, c), way, col_sem).start()
            else:
                part = c * UNITS // CHUNKS
                start = part * (reads // UNITS)
                held = (left if kind == 0 else right).at[pl.ds((row_tile if kind == 0 else col_tile)[s] + start, reads // UNITS)]
                target = right.at[pl.ds(col_tile[s] + start, reads // UNITS)]
                copy(held, target, CORE, core_sem).start()
                if kind == 0:
                    target[...] = held[...]

    sent = {}

    def run_slot(slot):
        for kind, role, entries in SLOTS[slot]:
            for entry in entries:
                for way in entry[2:]:
                    at = (0 if way <= ZH else 1, role, way)
                    sent[at] = sent.get(at, 0) + 1

            @pl.when((row_place if kind == 0 else col_place) == role)
            def _(kind=kind, role=role, entries=entries):
                for entry in entries:
                    handle(kind, role, entry[0], entry[1], entry[2:])

    def dispatch(slot, low, high):
        if high - low == 1:
            run_slot(low)
            return
        middle = (low + high) // 2

        @pl.when(slot < middle)
        def _():
            dispatch(slot, low, middle)

        @pl.when(slot >= middle)
        def _():
            dispatch(slot, middle, high)

    @pl.loop(0, len(SLOTS))
    def _(slot):
        dispatch(slot, 0, len(SLOTS))

    for (kind, role, way), count in sorted(sent.items()):

        @pl.when((row_place if kind == 0 else col_place) == role)
        def _(way=way, count=count):
            block = right.at[pl.ds(0, 8 * reads if way == CORE else count * piece)]
            copy(block, block, way, core_sem).wait_send()
            if way == CORE:
                copy(block, block, way, core_sem).wait_recv()


def gather(tile_pattern, weights):
    reads, bins = weights.shape
    return pl.pallas_call(
        gather_kernel,
        out_shape=(pltpu.VMEM((8 * reads, bins), weights.dtype), pltpu.VMEM((16 * reads, bins), weights.dtype)),
        in_specs=[pl.BlockSpec(memory_space=pltpu.HBM), pl.BlockSpec(memory_space=pltpu.HBM)],
        out_specs=(pl.BlockSpec(memory_space=pltpu.VMEM),) * 2,
        scratch_shapes=[
            pltpu.SMEM(tile_pattern.shape, tile_pattern.dtype),
            pltpu.VMEM(weights.shape, weights.dtype),
            pltpu.SemaphoreType.DMA((2,)),
            pltpu.SemaphoreType.DMA((7,)),
            pltpu.SemaphoreType.DMA((8, CHUNKS)),
            pltpu.SemaphoreType.DMA((8, CHUNKS)),
            pltpu.SemaphoreType.DMA,
        ],
        compiler_params=pltpu.CompilerParams(collective_id=0, has_side_effects=True, vmem_limit_bytes=8 << 20),
        name="gather",
    )(*[pltpu.with_memory_space_constraint(a, pltpu.HBM) for a in (tile_pattern, weights)])


def product_kernel(scale, left, right, out, full, stage, sems):
    row, col = lax.axis_index("row"), lax.axis_index("col")
    slots, _, tile = stage.shape
    section_count = full.shape[1]
    bin_tile = left.shape[1] // section_count
    rows, cols = left.shape[0] // tile, right.shape[0] // tile

    def tile_at(index):
        return pl.ds(pl.multiple_of(index * tile, tile), tile)

    def write(j, slot):
        return pltpu.make_async_copy(stage.at[slot], out.at[:, tile_at(j)], sems.at[slot])

    for j in range(cols):
        for s in range(section_count):
            part = jnp.abs(right[pl.ds(j * tile, tile), pl.ds(s * bin_tile, bin_tile)]).reshape(-1, 16, bin_tile)
            top = jnp.max(jnp.max(part, axis=0).astype(jnp.float32))
            full[j, s] = (top > 0.0).astype(jnp.int32)

    @pl.loop(0, cols)
    def _(j):
        slot = lax.rem(j, slots)

        @pl.when(j >= slots)
        def _():
            write(j - slots, slot).wait()

        case = full[j, 0] + 2 * full[j, 1]

        def put(part):
            stage[slot] = (dot(left[:, part], right[tile_at(j), part]) * scale).astype(stage.dtype)

        @pl.when(case == 0)
        def _():
            stage[slot] = jnp.zeros(stage.shape[1:], stage.dtype)

        @pl.when(case == 1)
        def _():
            put(pl.ds(0, bin_tile))

        @pl.when(case == 2)
        def _():
            put(pl.ds(bin_tile, bin_tile))

        @pl.when(case == 3)
        def _():
            put(pl.ds(0, 2 * bin_tile))

        i = col * cols + j - row * rows

        @pl.when(jnp.logical_and(i >= 0, i < rows))
        def _():
            stage[slot, tile_at(i), :] = clear_diagonal(stage[slot, tile_at(i), :])

        write(j, slot).start()

    for j in range(cols - slots, cols):
        write(j, j % slots).wait()


def product(left, right, section_count):
    rows, cols = left.shape[0], right.shape[0]
    tile = rows // 8
    slots = 8

    def kernel(*refs):
        product_kernel(1.0 / math.sqrt(left.shape[1]), *refs)

    return pl.pallas_call(
        kernel,
        out_shape=jax.ShapeDtypeStruct((rows, cols), left.dtype),
        in_specs=[pl.BlockSpec(memory_space=pltpu.VMEM)] * 2,
        out_specs=pl.BlockSpec(memory_space=pl.ANY),
        scratch_shapes=[
            pltpu.SMEM((cols // tile, section_count), jnp.int32),
            pltpu.VMEM((slots, rows, tile), left.dtype),
            pltpu.SemaphoreType.DMA((slots,)),
        ],
        compiler_params=pltpu.CompilerParams(vmem_limit_bytes=24 << 20),
        name="product",
    )(left, right)


def shards(weights, tile_pattern):
    return product(*gather(tile_pattern, weights), tile_pattern.shape[1])


def solution(mesh):
    return jax.shard_map(
        shards,
        mesh=mesh,
        in_specs=(P(("row", "col"), None), P(("row", "col"), None)),
        out_specs=P("row", "col"),
        check_vma=False,
    )
```
